512 devices in a mesh: rows: 128 (over z, y, core), freq: 4 (over x).
Axes of the slice: x: 4, y: 4, z: 16, core: 2. Of those that a mesh axis runs over, the one named last changes fastest.
Arguments:
- correlation: bfloat16 [2, 128, 4, 512, 1024], P(None, 'rows', None, None, 'freq'), may hold values from -1500 to 1500
- band_tiles: int32 [128, 4], P('rows'), may hold values from 0 to 130, as said below
Outputs:
- coherence: bfloat16 [2, 128, 3, 1024, 512], P(None, 'rows', None, 'freq')
The draws below stay inside these ranges and needn't reach their ends.
Inputs may be any that keep to these rules, and one draw needn't show every extreme that they name: band_tiles[a, :] lists in increasing order the 4 live tiles with index at or after a; a tile is live for every row or for none; tiles 0 and 127 and all tiles from 128 on are live.
All inputs are finite; a program needn't handle non-finite values.
Results may differ from the reference program's by a relative error of at most 0.001.
Values may be sent and summed in bfloat16 or wider, within the bound.
No kernel may reach another device: no remote copies, remote signals or barrier semaphores. Data moves between devices by JAX's collectives and lax.ppermute only.
A program may use at most 64 MiB of HBM per device.

```python
import math
import jax
import jax.numpy as jnp
from jax import lax

TS = 512
NB = 2
BAND = 4
NE = 3
NTR = 128


def draw_band_tiles(key, part):
    span_tiles = NTR + BAND
    dead_tiles = jax.random.randint(key, (span_tiles,), 0, 2) == 0
    positions = jnp.arange(span_tiles)
    forced = (positions == 0) | (positions >= NTR - 1)
    live_tiles = jnp.where(forced | jnp.logical_not(dead_tiles), 1, 0).astype(jnp.int32)
    running = jnp.cumsum(live_tiles)
    earlier = running - live_tiles
    targets = earlier[:NTR][:, None] + jnp.arange(BAND, dtype=jnp.int32)[None, :] + 1
    return jnp.sum((running[None, None, :] < targets[:, :, None]).astype(jnp.int32), axis=2).astype(jnp.int32)


def draw_correlation(key, part):
    shape = (2, NTR, BAND, TS, NB * TS)
    first, second, third = jax.random.split(key, 3)
    columns = (jnp.arange(NB * TS) % TS).astype(jnp.float32)
    ramp = jnp.sqrt(1.0 + 8.0 * columns / TS)
    values = jnp.clip(jax.random.normal(first, shape, jnp.float32), -4.0, 4.0)
    row_scale = jnp.exp(jax.random.uniform(second, (1, NTR, BAND, TS, 1), jnp.float32, 0.0, math.log(10.0)))
    column_scale = jnp.exp(jax.random.uniform(third, (1, 1, 1, 1, NB * TS), jnp.float32, 0.0, math.log(10.0))) * ramp
    return (values * row_scale * column_scale).astype(jnp.bfloat16)


def setup_inputs(seed: int = 0) -> dict:
    key_list = jax.random.split(jax.random.key(seed), 3)
    return {
        "correlation": draw_correlation(jax.random.fold_in(key_list[2], 71), 0),
        "band_tiles": draw_band_tiles(jax.random.fold_in(key_list[2], 71), 0),
    }


EPSILON = 1e-06

def reference(correlation, band_tiles):
    squares = jnp.square(correlation.astype(jnp.float32)).reshape(2, NTR, BAND, TS, NB, TS)
    energy = lax.optimization_barrier(jnp.sum(squares, axis=(0, 2, 5)))

    def one_row(row_index):
        left_tiles = lax.dynamic_index_in_dim(correlation, row_index, 1, keepdims=False)
        left_tiles = left_tiles.astype(jnp.float32).reshape(2, BAND, TS, NB, TS)
        own_sources = lax.dynamic_index_in_dim(band_tiles, row_index, 0, keepdims=False)
        own_energy = lax.dynamic_index_in_dim(energy, row_index, 0, keepdims=False)
        results = []
        for offset in range(NE):
            far_index = row_index + offset
            valid = far_index < NTR
            clamped = jnp.minimum(far_index, NTR - 1).astype(jnp.int32)
            far_tiles = lax.dynamic_index_in_dim(correlation, clamped, 1, keepdims=False)
            far_tiles = far_tiles.astype(jnp.float32).reshape(2, BAND, TS, NB, TS)
            far_sources = lax.dynamic_index_in_dim(band_tiles, clamped, 0, keepdims=False)
            far_sources = jnp.where(valid, far_sources, jnp.full_like(far_sources, -1))
            far_energy = lax.dynamic_index_in_dim(energy, clamped, 0, keepdims=False)
            far_energy = jnp.where(valid, far_energy, jnp.zeros_like(far_energy))
            matches = (own_sources[:, None] == far_sources[None, :]).astype(jnp.float32)
            aligned = jnp.einsum('dk,rkqbc->rdqbc', matches, far_tiles)
            real_part = jnp.einsum('rdpbc,rdqbc->bpq', left_tiles, aligned)
            imag_part = jnp.einsum('dpbc,dqbc->bpq', left_tiles[1], aligned[0]) - jnp.einsum('dpbc,dqbc->bpq', left_tiles[0], aligned[1])
            denominator = own_energy.T[:, :, None] * far_energy.T[:, None, :] + EPSILON
            scaled = jnp.stack([real_part, imag_part]) * lax.rsqrt(denominator)[None]
            results.append(scaled.astype(jnp.bfloat16))
        return jnp.stack(results, axis=1)
    mapped = lax.map(one_row, jnp.arange(NTR, dtype=jnp.int32))
    return jnp.transpose(mapped, (1, 0, 2, 3, 4, 5)).reshape(2, NTR, NE, NB * TS, TS)
```

```python
import jax
import jax.numpy as jnp
from jax import lax
from jax.experimental import pallas as pl
from jax.experimental.pallas import tpu as pltpu
from jax.sharding import PartitionSpec as P

TS = 512
HALF = 256
BAND = 4
CHUNKS = 2
CR = HALF // CHUNKS
EPSILON = 1e-06
CODE = 2.0**7.5
VMEM = pl.BlockSpec(memory_space=pltpu.VMEM)
ANY = pl.BlockSpec(memory_space=pl.ANY)
SMEM = pl.BlockSpec(memory_space=pltpu.SMEM)
PARAMS = pltpu.CompilerParams(vmem_limit_bytes=40 * 1024 * 1024)


def encode(x):
    u = x * CODE
    y = u * u
    y = y * y
    y = y * y
    y = y * y
    return jnp.where(u < 0, -y, y).astype(jnp.bfloat16)


def decode(y):
    y = y.astype(jnp.float32)
    r = lax.rsqrt(lax.rsqrt(lax.rsqrt(lax.rsqrt(jnp.abs(y))))) * (1.0 / CODE)
    return jnp.where(y < 0, -r, r)


def column(row):
    width = row.shape[1]
    return jnp.transpose(jnp.broadcast_to(row, (128, width)))


def complex_product(left, right_re, right_im):
    dims = (((1,), (1,)), ((), ()))
    with_re = lax.dot_general(left, right_re, dims, preferred_element_type=jnp.float32)
    with_im = lax.dot_general(left, right_im, dims, preferred_element_type=jnp.float32)
    rows = left.shape[0] // 2
    return with_re[:rows] + with_im[rows:], with_re[rows:] - with_im[:rows]


def pack_kernel(own_ref, band_ref, chunk0_ref, chunk1_ref, msg_ref):
    chunks = (chunk0_ref, chunk1_ref)
    msg_ref[...] = jnp.zeros_like(msg_ref)
    for d in range(BAND):
        msg_ref[1 + d : 2 + d, :] = jnp.full((1, TS), band_ref[0, d].astype(jnp.float32))
    for half in range(2):
        for j in range(CHUNKS):
            start = half * HALF + j * CR
            total = jnp.zeros((CR, HALF), jnp.float32)
            for part in range(2):
                for d in range(BAND):
                    block = own_ref[part, d, start : start + CR, :]
                    chunks[j][part, d, half] = block
                    wide = block.astype(jnp.float32)
                    total += wide * wide
            folded = jnp.transpose(total[:, :128] + total[:, 128:])
            msg_ref[0:1, start : start + CR] = jnp.sum(folded, axis=0, keepdims=True)


def self_kernel(pos_ref, own_ref, msg_ref, kept_ref, given_ref, col_ref):
    mine = pos_ref[1]
    row = msg_ref[0:1, :]
    col_ref[...] = column(row)
    right_re = jnp.concatenate([own_ref[0, d] for d in range(BAND)], axis=1)
    right_im = jnp.concatenate([own_ref[1, d] for d in range(BAND)], axis=1)
    for keep in (False, True):
        start = pl.multiple_of((mine if keep else 1 - mine) * HALF, HALF)
        left = jnp.concatenate(
            [
                jnp.concatenate(
                    [own_ref[part, d, pl.ds(start, HALF), :] for d in range(BAND)], axis=1
                )
                for part in range(2)
            ],
            axis=0,
        )
        real, imag = complex_product(left, right_re, right_im)
        scale = lax.rsqrt(col_ref[pl.ds(start, HALF), 0:1] * row + EPSILON)
        if keep:
            kept_ref[0] = real * scale
            kept_ref[1] = imag * scale
        else:
            given_ref[0] = encode(real * scale)
            given_ref[1] = encode(imag * scale)


def pair_kernel(
    j, pos_ref, own_s, near_s, far_s, own_ref, near_ref, far_ref, own_m, near_m, far_m,
    kept_ref, given_ref, col_ref,
):
    core = pos_ref[0]
    mine = pos_ref[1]

    def shift(left_s, right_s):
        first = right_s[1, 0]
        return sum((left_s[1 + d, 0] < first).astype(jnp.int32) for d in range(BAND))

    def aligned(load, part, s):
        blocks = []
        for d in range(BAND):
            block = load(part, jnp.maximum(d - s, 0))
            if d < 2:
                block = jnp.where(d >= s, block, jnp.zeros_like(block))
            blocks.append(block)
        return jnp.concatenate(blocks, axis=1)

    def chunk_of_rows(ref):
        def load(part, k):
            return jnp.concatenate(
                [ref[part, k, h * HALF + j * CR : h * HALF + j * CR + CR, :] for h in range(2)],
                axis=0,
            )
        return load

    def chunk_of_lanes(ref):
        return jnp.concatenate(
            [ref[0:1, h * HALF + j * CR : h * HALF + j * CR + CR] for h in range(2)], axis=1
        )

    def emit(unit, keep, real, imag, scale, split):
        for part, value in enumerate((real, imag)):
            value = value * scale
            for tile in range(2):
                piece = split(value, tile)
                if keep:
                    kept_ref[unit, part, tile] = piece
                else:
                    given_ref[unit, part, tile] = encode(piece)

    @pl.when(core == 0)
    def _():
        col_ref[...] = column(own_m[0:1, :])
        units = (
            (near_s, chunk_of_rows(near_ref), near_m),
            (far_s, lambda part, k: far_ref[part, k].reshape(2 * CR, HALF), far_m),
        )
        for unit, (right_s, load, right_m) in enumerate(units):
            s = shift(own_s, right_s)
            right_re = aligned(load, 0, s)
            right_im = aligned(load, 1, s)
            row = chunk_of_lanes(right_m)
            for keep in (False, True):
                start = pl.multiple_of((mine if keep else 1 - mine) * HALF, HALF)
                left = jnp.concatenate(
                    [
                        jnp.concatenate(
                            [own_ref[part, d, pl.ds(start, HALF), :] for d in range(BAND)], axis=1
                        )
                        for part in range(2)
                    ],
                    axis=0,
                )
                real, imag = complex_product(left, right_re, right_im)
                scale = lax.rsqrt(col_ref[pl.ds(start, HALF), 0:1] * row + EPSILON)
                emit(unit, keep, real, imag, scale, lambda v, t: v[t * CR : t * CR + CR])

    @pl.when(core == 1)
    def _():
        col_ref[...] = column(far_m[0:1, :])
        units = ((near_s, near_ref, near_m), (own_s, own_ref, own_m))
        for unit, (right_s, right_ref, right_m) in enumerate(units):
            s = shift(far_s, right_s)
            load = lambda part, k: right_ref[part, k]
            right_re = aligned(load, 0, s)
            right_im = aligned(load, 1, s)
            row = right_m[0:1, :]
            for keep in (False, True):
                half = mine if keep else 1 - mine
                left = jnp.concatenate(
                    [
                        jnp.concatenate([far_ref[part, d, half] for d in range(BAND)], axis=1)
                        for part in range(2)
                    ],
                    axis=0,
                )
                real, imag = complex_product(left, right_re, right_im)
                start = pl.multiple_of(half * HALF + j * CR, CR)
                scale = lax.rsqrt(col_ref[pl.ds(start, CR), 0:1] * row + EPSILON)
                emit(unit, keep, real, imag, scale, lambda v, t: v[:, t * HALF : t * HALF + HALF])


def self_finish_kernel(kept_ref, got_ref, out_ref, token_ref, fin_ref, sem):
    token_ref[...] = jnp.zeros_like(token_ref)
    for part in range(2):
        fin_ref[part] = (kept_ref[part] + decode(got_ref[part])).astype(jnp.bfloat16)
    copies = [
        pltpu.make_async_copy(fin_ref.at[part], out_ref.at[part, 0, 0], sem.at[part])
        for part in range(2)
    ]
    for copy in copies:
        copy.start()
    for copy in copies:
        copy.wait()


def pair_finish_kernel(kept_ref, got_ref, fin_ref):
    for unit in range(2):
        for part in range(2):
            for tile in range(2):
                value = kept_ref[unit, part, tile] + decode(got_ref[unit, part, tile])
                fin_ref[unit, part, tile] = value.astype(jnp.bfloat16)


def place_kernel(j, pos_ref, out_in_ref, fin_ref, back_ref, out_ref, sem):
    del out_in_ref
    rows = pl.ds(j * CR, CR)
    pieces = [(unit, part, tile) for unit in range(2) for part in range(2) for tile in range(2)]

    def run(copies):
        for copy in copies:
            copy.start()
        for copy in copies:
            copy.wait()

    @pl.when(pos_ref[0] == 0)
    def _():
        run(
            [
                pltpu.make_async_copy(
                    fin_ref.at[unit, part, tile, :, pl.ds(h * CR, CR)],
                    out_ref.at[
                        part, 0, 1 + unit, pl.ds(tile * CR, CR), pl.ds(h * HALF + j * CR, CR)
                    ],
                    sem.at[2 * i + h],
                )
                for i, (unit, part, tile) in enumerate(pieces)
                for h in range(2)
            ]
        )

    @pl.when(pos_ref[0] == 1)
    def _():
        run(
            [
                pltpu.make_async_copy(
                    back_ref.at[unit, part, tile],
                    out_ref.at[part, 0, 1 + unit, rows, pl.ds(tile * HALF, HALF)],
                    sem.at[i],
                )
                for i, (unit, part, tile) in enumerate(pieces)
            ]
        )


def call(kernel, outs, specs, scratch=(), flops=0, after=None, out_specs=None, aliases=None):
    shapes = [jax.ShapeDtypeStruct(shape, dtype) for shape, dtype in outs]
    body = kernel if after is None else lambda _, *refs: kernel(*refs)
    run = pl.pallas_call(
        body,
        out_shape=shapes if len(shapes) > 1 else shapes[0],
        in_specs=specs if after is None else [ANY, *specs],
        out_specs=out_specs or ([VMEM] * len(shapes) if len(shapes) > 1 else VMEM),
        scratch_shapes=list(scratch),
        compiler_params=PARAMS,
        input_output_aliases=aliases or {},
        cost_estimate=pl.CostEstimate(flops=flops, bytes_accessed=2**21, transcendentals=0),
    )
    return run if after is None else lambda *args: run(after, *args)


def shards(correlation, band_tiles):
    bf16, f32 = jnp.bfloat16, jnp.float32
    count = lax.axis_size("rows")
    core = lax.axis_index("rows") % 2
    mine = lax.axis_index("freq") % 2
    pos = jnp.stack([core, mine]).astype(jnp.int32)
    own = correlation.reshape(2, BAND, TS, HALF)
    swap = [(i, i ^ 1) for i in range(lax.axis_size("freq"))]
    pair = [(i, i ^ 1) for i in range(count)]
    far_route = [(i + 2, i) for i in range(0, count - 2, 2)] + [(i - 2, i) for i in range(3, count, 2)]
    back_route = [(i, i - 2) for i in range(3, count, 2)]

    chunk_shape = (2, BAND, 2, CR, HALF)
    chunk0, chunk1, my_energy = call(
        pack_kernel,
        [(chunk_shape, bf16), (chunk_shape, bf16), ((8, TS), f32)],
        [VMEM, SMEM],
    )(own, band_tiles)
    far = [lax.ppermute(chunk, "rows", far_route) for chunk in (chunk0, chunk1)]
    near = lax.ppermute(own, "rows", pair)
    message = my_energy + lax.ppermute(my_energy, "freq", swap)
    near_message = lax.ppermute(message, "rows", pair)
    far_message = lax.ppermute(message, "rows", far_route)
    kept_self, given_self = call(
        self_kernel,
        [((2, HALF, TS), f32), ((2, HALF, TS), bf16)],
        [SMEM, VMEM, VMEM],
        [pltpu.VMEM((TS, 128), f32)],
    )(pos, own, message)
    got_self = lax.ppermute(given_self, "freq", swap)

    unit_shape = (2, 2, 2, CR, HALF)
    after = kept_self
    out, products = None, []
    for j in range(CHUNKS):
        kept, given = call(
            lambda *refs, j=j: pair_kernel(j, *refs),
            [(unit_shape, f32), (unit_shape, bf16)],
            [SMEM] * 4 + [VMEM] * 6,
            [pltpu.VMEM((TS, 128), f32)],
            flops=2**28,
            after=after,
        )(pos, message, near_message, far_message, own, near, far[j], message, near_message, far_message)
        got = lax.ppermute(given, "freq", swap)
        if j == 0:
            out, after = call(
                self_finish_kernel,
                [((2, 1, 3, HALF, TS), bf16), ((8, 128), f32)],
                [VMEM, VMEM],
                [pltpu.VMEM((2, HALF, TS), bf16), pltpu.SemaphoreType.DMA((2,))],
                after=kept,
                out_specs=[ANY, VMEM],
            )(kept_self, got_self)
        products.append((kept, got))
    for j, (kept, got) in enumerate(products):
        fin = call(pair_finish_kernel, [(unit_shape, bf16)], [VMEM, VMEM], after=after)(kept, got)
        after = fin
        back = lax.ppermute(fin, "rows", back_route)
        out = call(
            lambda *refs, j=j: place_kernel(j, *refs),
            [((2, 1, 3, HALF, TS), bf16)],
            [SMEM, ANY, VMEM, VMEM],
            [pltpu.SemaphoreType.DMA((16,))],
            out_specs=ANY,
            aliases={1: 0},
        )(pos, out, fin, back)
    return out


def solution(mesh):
    return jax.shard_map(
        shards,
        mesh=mesh,
        in_specs=(P(None, "rows", None, None, "freq"), P("rows", None)),
        out_specs=P(None, "rows", None, "freq", None),
        check_vma=False,
    )
```

```python
import jax
import jax.numpy as jnp
from jax import lax
from jax.experimental import pallas as pl
from jax.experimental.pallas import tpu as pltpu
from jax.sharding import PartitionSpec as P

TS = 512
HALF = 256
BAND = 4
CHUNKS = 2
CR = HALF // CHUNKS
EPSILON = 1e-06
TINY = 1e-30
CODE = 2.0**7.5
VMEM = pl.BlockSpec(memory_space=pltpu.VMEM)
ANY = pl.BlockSpec(memory_space=pl.ANY)
SMEM = pl.BlockSpec(memory_space=pltpu.SMEM)
MIB = 1024 * 1024
MCOST = 2**33
PCOST = 0
TCOST = 0
FCOST = 2**36


def encode(x):
    u = x * CODE
    y = u * u
    y = y * y
    y = y * y
    y = y * y
    return jnp.where(u < 0, -y, y).astype(jnp.bfloat16)


def decode(y):
    y = y.astype(jnp.float32)
    r = lax.rsqrt(lax.rsqrt(lax.rsqrt(lax.rsqrt(jnp.abs(y))))) * (1.0 / CODE)
    return jnp.where(y < 0, -r, r)


def column(row):
    width = row.shape[1]
    return jnp.transpose(jnp.broadcast_to(row, (128, width)))


def complex_product(left, right_re, right_im):
    dims = (((1,), (1,)), ((), ()))
    with_re = lax.dot_general(left, right_re, dims, preferred_element_type=jnp.float32)
    with_im = lax.dot_general(left, right_im, dims, preferred_element_type=jnp.float32)
    rows = left.shape[0] // 2
    return with_re[:rows] + with_im[rows:], with_re[rows:] - with_im[:rows]


def chunk_copies(j, own_ref, chunk_ref, sem):
    return [
        pltpu.make_async_copy(
            own_ref.at[:, :, pl.ds(half * HALF + j * CR, CR), :],
            chunk_ref.at[:, :, half],
            sem.at[half],
        )
        for half in range(2)
    ]


def pack_kernel(own_ref, chunk_ref, token_ref, sem):
    copies = chunk_copies(0, own_ref, chunk_ref, sem)
    for copy in copies:
        copy.start()
    token_ref[...] = jnp.zeros_like(token_ref)
    for copy in copies:
        copy.wait()


def order_kernel(_, token_ref):
    token_ref[...] = jnp.zeros_like(token_ref)


def message_kernel(own_ref, mine_ref, other_ref, msg_ref, chunk_ref, sem):
    copies = chunk_copies(1, own_ref, chunk_ref, sem)
    for copy in copies:
        copy.start()
    msg_ref[...] = mine_ref[...] + other_ref[...]
    for copy in copies:
        copy.wait()


def self_kernel(pos_ref, band_ref, own_ref, kept_ref, given_ref, msg_ref, product_ref, col_ref):
    mine = pos_ref[1]
    msg_ref[...] = jnp.zeros_like(msg_ref)
    for d in range(BAND):
        msg_ref[1 + d : 2 + d, :] = jnp.full((1, TS), band_ref[0, d].astype(jnp.float32))
    right_re = jnp.concatenate([own_ref[0, d] for d in range(BAND)], axis=1)
    right_im = jnp.concatenate([own_ref[1, d] for d in range(BAND)], axis=1)
    diagonal = lax.broadcasted_iota(jnp.int32, (HALF, HALF), 0) == lax.broadcasted_iota(
        jnp.int32, (HALF, HALF), 1
    )
    for half in range(2):
        start = half * HALF
        left = jnp.concatenate(
            [
                jnp.concatenate(
                    [own_ref[part, d, start : start + HALF, :] for d in range(BAND)], axis=1
                )
                for part in range(2)
            ],
            axis=0,
        )
        real, imag = complex_product(left, right_re, right_im)
        product_ref[half, 0] = real
        product_ref[half, 1] = imag
        energies = jnp.where(diagonal, real[:, start : start + HALF], 0.0)
        msg_ref[0:1, start : start + HALF] = jnp.sum(energies, axis=0, keepdims=True)
        col_ref[start : start + HALF, :] = jnp.broadcast_to(
            jnp.sum(energies, axis=1, keepdims=True), (HALF, 128)
        )
    other = pl.multiple_of((1 - mine) * HALF, HALF)
    scale = lax.rsqrt(jnp.maximum(col_ref[pl.ds(other, HALF), 0:1], TINY)) * lax.rsqrt(
        jnp.maximum(msg_ref[0:1, :], TINY)
    )
    for part in range(2):
        given_ref[part] = encode(product_ref[1 - mine, part] * scale)
        kept_ref[part] = product_ref[mine, part]


def pair_kernel(
    j, pos_ref, own_s, near_s, far_s, own_ref, near_ref, far_ref, own_m, near_m, far_m,
    kept_ref, given_ref, col_ref,
):
    core = pos_ref[0]
    mine = pos_ref[1]

    def shift(left_s, right_s):
        first = right_s[1, 0]
        return sum((left_s[1 + d, 0] < first).astype(jnp.int32) for d in range(BAND))

    def aligned(load, part, s):
        blocks = []
        for d in range(BAND):
            block = load(part, jnp.maximum(d - s, 0))
            if d < 2:
                block = jnp.where(d >= s, block, jnp.zeros_like(block))
            blocks.append(block)
        return jnp.concatenate(blocks, axis=1)

    def chunk_of_rows(ref):
        def load(part, k):
            return jnp.concatenate(
                [ref[part, k, h * HALF + j * CR : h * HALF + j * CR + CR, :] for h in range(2)],
                axis=0,
            )
        return load

    def chunk_of_lanes(ref):
        return jnp.concatenate(
            [ref[0:1, h * HALF + j * CR : h * HALF + j * CR + CR] for h in range(2)], axis=1
        )

    def emit(unit, keep, real, imag, scale, split):
        for part, value in enumerate((real, imag)):
            value = value * scale
            for tile in range(2):
                piece = split(value, tile)
                if keep:
                    kept_ref[unit, part, tile] = piece
                else:
                    given_ref[unit, part, tile] = encode(piece)

    @pl.when(core == 0)
    def _():
        col_ref[...] = column(own_m[0:1, :])
        units = (
            (near_s, chunk_of_rows(near_ref), near_m),
            (far_s, lambda part, k: far_ref[part, k].reshape(2 * CR, HALF), far_m),
        )
        for unit, (right_s, load, right_m) in enumerate(units):
            s = shift(own_s, right_s)
            right_re = aligned(load, 0, s)
            right_im = aligned(load, 1, s)
            row = chunk_of_lanes(right_m)
            for keep in (False, True):
                start = pl.multiple_of((mine if keep else 1 - mine) * HALF, HALF)
                left = jnp.concatenate(
                    [
                        jnp.concatenate(
                            [own_ref[part, d, pl.ds(start, HALF), :] for d in range(BAND)], axis=1
                        )
                        for part in range(2)
                    ],
                    axis=0,
                )
                real, imag = complex_product(left, right_re, right_im)
                scale = lax.rsqrt(col_ref[pl.ds(start, HALF), 0:1] * row + EPSILON)
                emit(unit, keep, real, imag, scale, lambda v, t: v[t * CR : t * CR + CR])

    @pl.when(core == 1)
    def _():
        col_ref[...] = column(far_m[0:1, :])
        units = ((near_s, near_ref, near_m), (own_s, own_ref, own_m))
        for unit, (right_s, right_ref, right_m) in enumerate(units):
            s = shift(far_s, right_s)
            load = lambda part, k: right_ref[part, k]
            right_re = aligned(load, 0, s)
            right_im = aligned(load, 1, s)
            row = right_m[0:1, :]
            for keep in (False, True):
                half = mine if keep else 1 - mine
                left = jnp.concatenate(
                    [
                        jnp.concatenate([far_ref[part, d, half] for d in range(BAND)], axis=1)
                        for part in range(2)
                    ],
                    axis=0,
                )
                real, imag = complex_product(left, right_re, right_im)
                start = pl.multiple_of(half * HALF + j * CR, CR)
                scale = lax.rsqrt(col_ref[pl.ds(start, CR), 0:1] * row + EPSILON)
                emit(unit, keep, real, imag, scale, lambda v, t: v[:, t * HALF : t * HALF + HALF])


def self_finish_kernel(
    pos_ref, kept_ref, got_ref, mine_ref, other_ref, out_ref, token_ref, fin_ref, col_ref, sem
):
    token_ref[...] = jnp.zeros_like(token_ref)
    start = pl.multiple_of(pos_ref[1] * HALF, HALF)
    other = jnp.sqrt(jnp.maximum(other_ref[0:1, :], TINY))
    total = mine_ref[0:1, :] + other_ref[0:1, :]
    col_ref[0] = column(other)
    col_ref[1] = column(total)
    scale = lax.rsqrt(col_ref[1, pl.ds(start, HALF), 0:1] * total + EPSILON)
    back = col_ref[0, pl.ds(start, HALF), 0:1] * other
    for part in range(2):
        value = (kept_ref[part] + decode(got_ref[part]) * back) * scale
        fin_ref[part] = value.astype(jnp.bfloat16)
    copies = [
        pltpu.make_async_copy(fin_ref.at[part], out_ref.at[part, 0, 0], sem.at[part])
        for part in range(2)
    ]
    for copy in copies:
        copy.start()
    for copy in copies:
        copy.wait()


def pair_finish_kernel(kept_ref, got_ref, fin_ref):
    for unit in range(2):
        for part in range(2):
            for tile in range(2):
                value = kept_ref[unit, part, tile] + decode(got_ref[unit, part, tile])
                fin_ref[unit, part, tile] = value.astype(jnp.bfloat16)


def place_kernel(j, pos_ref, out_in_ref, fin_ref, back_ref, out_ref, sem):
    del out_in_ref
    rows = pl.ds(j * CR, CR)
    pieces = [(unit, part, tile) for unit in range(2) for part in range(2) for tile in range(2)]

    def run(copies):
        for copy in copies:
            copy.start()
        for copy in copies:
            copy.wait()

    @pl.when(pos_ref[0] == 0)
    def _():
        run(
            [
                pltpu.make_async_copy(
                    fin_ref.at[unit, part, tile, :, pl.ds(h * CR, CR)],
                    out_ref.at[
                        part, 0, 1 + unit, pl.ds(tile * CR, CR), pl.ds(h * HALF + j * CR, CR)
                    ],
                    sem.at[2 * i + h],
                )
                for i, (unit, part, tile) in enumerate(pieces)
                for h in range(2)
            ]
        )

    @pl.when(pos_ref[0] == 1)
    def _():
        run(
            [
                pltpu.make_async_copy(
                    back_ref.at[unit, part, tile],
                    out_ref.at[part, 0, 1 + unit, rows, pl.ds(tile * HALF, HALF)],
                    sem.at[i],
                )
                for i, (unit, part, tile) in enumerate(pieces)
            ]
        )


def call(name, kernel, outs, specs, scratch=(), flops=0, after=None, out_specs=None, aliases=None, vmem=40):
    shapes = [jax.ShapeDtypeStruct(shape, dtype) for shape, dtype in outs]
    body = kernel if after is None else lambda _, *refs: kernel(*refs)
    run = pl.pallas_call(
        body,
        name=name,
        out_shape=shapes if len(shapes) > 1 else shapes[0],
        in_specs=specs if after is None else [ANY, *specs],
        out_specs=out_specs or ([VMEM] * len(shapes) if len(shapes) > 1 else VMEM),
        scratch_shapes=list(scratch),
        compiler_params=pltpu.CompilerParams(vmem_limit_bytes=vmem * MIB),
        input_output_aliases=aliases or {},
        cost_estimate=pl.CostEstimate(flops=flops, bytes_accessed=2**21, transcendentals=0),
    )
    return run if after is None else lambda *args: run(after, *args)


def shards(correlation, band_tiles):
    bf16, f32 = jnp.bfloat16, jnp.float32
    count = lax.axis_size("rows")
    core = lax.axis_index("rows") % 2
    mine = lax.axis_index("freq") % 2
    pos = jnp.stack([core, mine]).astype(jnp.int32)
    own = correlation.reshape(2, BAND, TS, HALF)
    swap = [(i, i ^ 1) for i in range(lax.axis_size("freq"))]
    pair = [(i, i ^ 1) for i in range(count)]
    far_route = [(i + 2, i) for i in range(0, count - 2, 2)] + [(i - 2, i) for i in range(3, count, 2)]
    across_route = [(i + 3, i) for i in range(0, count - 2, 2)] + [(i - 3, i) for i in range(3, count, 2)]
    back_route = [(i, i - 2) for i in range(3, count, 2)]

    chunk_shape = (2, BAND, 2, CR, HALF)
    half_shape = (2, HALF, TS)
    token = ((8, 128), f32)
    chunk0, after = call(
        "pack",
        pack_kernel,
        [(chunk_shape, bf16), token],
        [ANY],
        [pltpu.SemaphoreType.DMA((2,))],
        out_specs=[ANY, VMEM],
        vmem=52,
    )(own)
    far0 = lax.ppermute(chunk0, "rows", far_route)
    kept_self, given_self, my_energy = call(
        "self",
        self_kernel,
        [(half_shape, f32), (half_shape, bf16), ((8, TS), f32)],
        [SMEM, SMEM, VMEM],
        [pltpu.VMEM((2, 2, HALF, TS), f32), pltpu.VMEM((TS, 128), f32)],
        after=after,
    )(pos, band_tiles, own)
    other_energy = lax.ppermute(my_energy, "freq", swap)
    got_self = lax.ppermute(given_self, "freq", swap)
    message, chunk1 = call(
        "message",
        message_kernel,
        [((8, TS), f32), (chunk_shape, bf16)],
        [VMEM] * 3,
        [pltpu.SemaphoreType.DMA((2,))],
        flops=MCOST,
    )(own, my_energy, other_energy)
    far1 = lax.ppermute(chunk1, "rows", far_route)
    near = lax.ppermute(own, "rows", pair)
    far = (far0, far1)
    near_message = lax.ppermute(message, "rows", pair)
    far_message = lax.ppermute(near_message, "rows", across_route)

    unit_shape = (2, 2, 2, CR, HALF)
    after = call("order", order_kernel, [token], [ANY], flops=TCOST)(far0)
    out, products = None, []
    for j in range(CHUNKS):
        kept, given = call(
            f"pair{j}",
            lambda *refs, j=j: pair_kernel(j, *refs),
            [(unit_shape, f32), (unit_shape, bf16)],
            [SMEM] * 4 + [VMEM] * 6,
            [pltpu.VMEM((TS, 128), f32)],
            flops=PCOST,
            after=after,
        )(pos, message, near_message, far_message, own, near, far[j], message, near_message, far_message)
        got = lax.ppermute(given, "freq", swap)
        if j == 0:
            out, after = call(
                "finish",
                self_finish_kernel,
                [((2, 1, 3, HALF, TS), bf16), token],
                [SMEM] + [VMEM] * 4,
                [
                    pltpu.VMEM((2, HALF, TS), bf16),
                    pltpu.VMEM((2, TS, 128), f32),
                    pltpu.SemaphoreType.DMA((2,)),
                ],
                flops=FCOST,
                after=kept,
                out_specs=[ANY, VMEM],
            )(pos, kept_self, got_self, my_energy, other_energy)
        products.append((kept, got))
    for j, (kept, got) in enumerate(products):
        fin = call("decode", pair_finish_kernel, [(unit_shape, bf16)], [VMEM, VMEM], after=after)(kept, got)
        after = fin
        back = lax.ppermute(fin, "rows", back_route)
        out = call(
            f"place{j}",
            lambda *refs, j=j: place_kernel(j, *refs),
            [((2, 1, 3, HALF, TS), bf16)],
            [SMEM, ANY, VMEM, VMEM],
            [pltpu.SemaphoreType.DMA((16,))],
            out_specs=ANY,
            aliases={1: 0},
        )(pos, out, fin, back)
    return out


def solution(mesh):
    return jax.shard_map(
        shards,
        mesh=mesh,
        in_specs=(P(None, "rows", None, None, "freq"), P("rows", None)),
        out_specs=P(None, "rows", None, "freq", None),
        check_vma=False,
    )
```

```python
import jax
import jax.numpy as jnp
from jax import lax
from jax.experimental import pallas as pl
from jax.experimental.pallas import tpu as pltpu
from jax.sharding import PartitionSpec as P

TS = 512
HALF = 256
BAND = 4
CHUNKS = 2
CR = HALF // CHUNKS
EPSILON = 1e-06
TINY = 1e-30
CODE = 2.0**7.5
VMEM = pl.BlockSpec(memory_space=pltpu.VMEM)
ANY = pl.BlockSpec(memory_space=pl.ANY)
SMEM = pl.BlockSpec(memory_space=pltpu.SMEM)
MIB = 1024 * 1024
MCOST = 2**33
PCOST = 0
TCOST = 0
FCOST = 2**36


def encode(x):
    u = x * CODE
    y = u * u
    y = y * y
    y = y * y
    y = y * y
    return jnp.where(u < 0, -y, y).astype(jnp.bfloat16)


def decode(y):
    y = y.astype(jnp.float32)
    r = lax.rsqrt(lax.rsqrt(lax.rsqrt(lax.rsqrt(jnp.abs(y))))) * (1.0 / CODE)
    return jnp.where(y < 0, -r, r)


def column(row):
    width = row.shape[1]
    return jnp.transpose(jnp.broadcast_to(row, (128, width)))


def complex_product(left, right_re, right_im):
    dims = (((1,), (1,)), ((), ()))
    with_re = lax.dot_general(left, right_re, dims, preferred_element_type=jnp.float32)
    with_im = lax.dot_general(left, right_im, dims, preferred_element_type=jnp.float32)
    rows = left.shape[0] // 2
    return with_re[:rows] + with_im[rows:], with_re[rows:] - with_im[:rows]


def chunk_copies(j, own_ref, chunk_ref, sem):
    return [
        pltpu.make_async_copy(
            own_ref.at[:, :, pl.ds(half * HALF + j * CR, CR), :],
            chunk_ref.at[:, :, half],
            sem.at[half],
        )
        for half in range(2)
    ]


def pack_kernel(own_ref, chunk0_ref, chunk1_ref, token_ref, sem):
    copies = chunk_copies(0, own_ref, chunk0_ref, sem.at[0])
    copies += chunk_copies(1, own_ref, chunk1_ref, sem.at[1])
    for copy in copies:
        copy.start()
    token_ref[...] = jnp.zeros_like(token_ref)
    for copy in copies:
        copy.wait()


def order_kernel(*refs):
    token_ref = refs[-1]
    token_ref[...] = jnp.zeros_like(token_ref)


def message_kernel(mine_ref, other_ref, msg_ref):
    msg_ref[...] = mine_ref[...] + other_ref[...]


def self_kernel(pos_ref, band_ref, own_ref, kept_ref, given_ref, msg_ref, product_ref, col_ref):
    mine = pos_ref[1]
    msg_ref[...] = jnp.zeros_like(msg_ref)
    for d in range(BAND):
        msg_ref[1 + d : 2 + d, :] = jnp.full((1, TS), band_ref[0, d].astype(jnp.float32))
    right_re = jnp.concatenate([own_ref[0, d] for d in range(BAND)], axis=1)
    right_im = jnp.concatenate([own_ref[1, d] for d in range(BAND)], axis=1)
    diagonal = lax.broadcasted_iota(jnp.int32, (HALF, HALF), 0) == lax.broadcasted_iota(
        jnp.int32, (HALF, HALF), 1
    )
    for half in range(2):
        start = half * HALF
        left = jnp.concatenate(
            [
                jnp.concatenate(
                    [own_ref[part, d, start : start + HALF, :] for d in range(BAND)], axis=1
                )
                for part in range(2)
            ],
            axis=0,
        )
        real, imag = complex_product(left, right_re, right_im)
        product_ref[half, 0] = real
        product_ref[half, 1] = imag
        energies = jnp.where(diagonal, real[:, start : start + HALF], 0.0)
        msg_ref[0:1, start : start + HALF] = jnp.sum(energies, axis=0, keepdims=True)
        col_ref[start : start + HALF, :] = jnp.broadcast_to(
            jnp.sum(energies, axis=1, keepdims=True), (HALF, 128)
        )
    other = pl.multiple_of((1 - mine) * HALF, HALF)
    scale = lax.rsqrt(jnp.maximum(col_ref[pl.ds(other, HALF), 0:1], TINY)) * lax.rsqrt(
        jnp.maximum(msg_ref[0:1, :], TINY)
    )
    for part in range(2):
        given_ref[part] = encode(product_ref[1 - mine, part] * scale)
        kept_ref[part] = product_ref[mine, part]


def pair_kernel(
    j, pos_ref, own_s, near_s, far_s, own_ref, near_ref, far_ref, own_m, near_m, far_m,
    kept_ref, given_ref, col_ref,
):
    core = pos_ref[0]
    mine = pos_ref[1]

    def shift(left_s, right_s):
        first = right_s[1, 0]
        return sum((left_s[1 + d, 0] < first).astype(jnp.int32) for d in range(BAND))

    def aligned(load, part, s):
        blocks = []
        for d in range(BAND):
            block = load(part, jnp.maximum(d - s, 0))
            if d < 2:
                block = jnp.where(d >= s, block, jnp.zeros_like(block))
            blocks.append(block)
        return jnp.concatenate(blocks, axis=1)

    def chunk_of_rows(ref):
        def load(part, k):
            return jnp.concatenate(
                [ref[part, k, h * HALF + j * CR : h * HALF + j * CR + CR, :] for h in range(2)],
                axis=0,
            )
        return load

    def chunk_of_lanes(ref):
        return jnp.concatenate(
            [ref[0:1, h * HALF + j * CR : h * HALF + j * CR + CR] for h in range(2)], axis=1
        )

    def emit(unit, keep, real, imag, scale, split):
        for part, value in enumerate((real, imag)):
            value = value * scale
            for tile in range(2):
                piece = split(value, tile)
                if keep:
                    kept_ref[unit, part, tile] = piece
                else:
                    given_ref[unit, part, tile] = encode(piece)

    @pl.when(core == 0)
    def _():
        col_ref[...] = column(own_m[0:1, :])
        units = (
            (near_s, chunk_of_rows(near_ref), near_m),
            (far_s, lambda part, k: far_ref[part, k].reshape(2 * CR, HALF), far_m),
        )
        for unit, (right_s, load, right_m) in enumerate(units):
            s = shift(own_s, right_s)
            right_re = aligned(load, 0, s)
            right_im = aligned(load, 1, s)
            row = chunk_of_lanes(right_m)
            for keep in (False, True):
                start = pl.multiple_of((mine if keep else 1 - mine) * HALF, HALF)
                left = jnp.concatenate(
                    [
                        jnp.concatenate(
                            [own_ref[part, d, pl.ds(start, HALF), :] for d in range(BAND)], axis=1
                        )
                        for part in range(2)
                    ],
                    axis=0,
                )
                real, imag = complex_product(left, right_re, right_im)
                scale = lax.rsqrt(col_ref[pl.ds(start, HALF), 0:1] * row + EPSILON)
                emit(unit, keep, real, imag, scale, lambda v, t: v[t * CR : t * CR + CR])

    @pl.when(core == 1)
    def _():
        col_ref[...] = column(far_m[0:1, :])
        units = ((near_s, near_ref, near_m), (own_s, own_ref, own_m))
        for unit, (right_s, right_ref, right_m) in enumerate(units):
            s = shift(far_s, right_s)
            load = lambda part, k: right_ref[part, k]
            right_re = aligned(load, 0, s)
            right_im = aligned(load, 1, s)
            row = right_m[0:1, :]
            for keep in (False, True):
                half = mine if keep else 1 - mine
                left = jnp.concatenate(
                    [
                        jnp.concatenate([far_ref[part, d, half] for d in range(BAND)], axis=1)
                        for part in range(2)
                    ],
                    axis=0,
                )
                real, imag = complex_product(left, right_re, right_im)
                start = pl.multiple_of(half * HALF + j * CR, CR)
                scale = lax.rsqrt(col_ref[pl.ds(start, CR), 0:1] * row + EPSILON)
                emit(unit, keep, real, imag, scale, lambda v, t: v[:, t * HALF : t * HALF + HALF])


def self_finish_kernel(
    pos_ref, kept_ref, got_ref, mine_ref, other_ref, out_ref, token_ref, fin_ref, col_ref, sem
):
    token_ref[...] = jnp.zeros_like(token_ref)
    start = pl.multiple_of(pos_ref[1] * HALF, HALF)
    other = jnp.sqrt(jnp.maximum(other_ref[0:1, :], TINY))
    total = mine_ref[0:1, :] + other_ref[0:1, :]
    col_ref[0] = column(other)
    col_ref[1] = column(total)
    scale = lax.rsqrt(col_ref[1, pl.ds(start, HALF), 0:1] * total + EPSILON)
    back = col_ref[0, pl.ds(start, HALF), 0:1] * other
    for part in range(2):
        value = (kept_ref[part] + decode(got_ref[part]) * back) * scale
        fin_ref[part] = value.astype(jnp.bfloat16)
    copies = [
        pltpu.make_async_copy(fin_ref.at[part], out_ref.at[part, 0, 0], sem.at[part])
        for part in range(2)
    ]
    for copy in copies:
        copy.start()
    for copy in copies:
        copy.wait()


def pair_finish_kernel(kept_ref, got_ref, fin_ref):
    for unit in range(2):
        for part in range(2):
            for tile in range(2):
                value = kept_ref[unit, part, tile] + decode(got_ref[unit, part, tile])
                fin_ref[unit, part, tile] = value.astype(jnp.bfloat16)


def place_kernel(j, pos_ref, out_in_ref, fin_ref, back_ref, out_ref, sem):
    del out_in_ref
    rows = pl.ds(j * CR, CR)
    pieces = [(unit, part, tile) for unit in range(2) for part in range(2) for tile in range(2)]

    def run(copies):
        for copy in copies:
            copy.start()
        for copy in copies:
            copy.wait()

    @pl.when(pos_ref[0] == 0)
    def _():
        run(
            [
                pltpu.make_async_copy(
                    fin_ref.at[unit, part, tile, :, pl.ds(h * CR, CR)],
                    out_ref.at[
                        part, 0, 1 + unit, pl.ds(tile * CR, CR), pl.ds(h * HALF + j * CR, CR)
                    ],
                    sem.at[2 * i + h],
                )
                for i, (unit, part, tile) in enumerate(pieces)
                for h in range(2)
            ]
        )

    @pl.when(pos_ref[0] == 1)
    def _():
        run(
            [
                pltpu.make_async_copy(
                    back_ref.at[unit, part, tile],
                    out_ref.at[part, 0, 1 + unit, rows, pl.ds(tile * HALF, HALF)],
                    sem.at[i],
                )
                for i, (unit, part, tile) in enumerate(pieces)
            ]
        )


def call(name, kernel, outs, specs, scratch=(), flops=0, after=None, out_specs=None, aliases=None, vmem=40):
    shapes = [jax.ShapeDtypeStruct(shape, dtype) for shape, dtype in outs]
    body = kernel if after is None else lambda _, *refs: kernel(*refs)
    run = pl.pallas_call(
        body,
        name=name,
        out_shape=shapes if len(shapes) > 1 else shapes[0],
        in_specs=specs if after is None else [ANY, *specs],
        out_specs=out_specs or ([VMEM] * len(shapes) if len(shapes) > 1 else VMEM),
        scratch_shapes=list(scratch),
        compiler_params=pltpu.CompilerParams(vmem_limit_bytes=vmem * MIB),
        input_output_aliases=aliases or {},
        cost_estimate=pl.CostEstimate(flops=flops, bytes_accessed=2**21, transcendentals=0),
    )
    return run if after is None else lambda *args: run(after, *args)


def shards(correlation, band_tiles):
    bf16, f32 = jnp.bfloat16, jnp.float32
    count = lax.axis_size("rows")
    core = lax.axis_index("rows") % 2
    mine = lax.axis_index("freq") % 2
    pos = jnp.stack([core, mine]).astype(jnp.int32)
    own = correlation.reshape(2, BAND, TS, HALF)
    swap = [(i, i ^ 1) for i in range(lax.axis_size("freq"))]
    pair = [(i, i ^ 1) for i in range(count)]
    far_route = [(i + 2, i) for i in range(0, count - 2, 2)] + [(i - 2, i) for i in range(3, count, 2)]
    across_route = [(i + 3, i) for i in range(0, count - 2, 2)] + [(i - 3, i) for i in range(3, count, 2)]
    back_route = [(i, i - 2) for i in range(3, count, 2)]

    chunk_shape = (2, BAND, 2, CR, HALF)
    half_shape = (2, HALF, TS)
    token = ((8, 128), f32)
    chunk0, chunk1, after = call(
        "pack",
        pack_kernel,
        [(chunk_shape, bf16), (chunk_shape, bf16), token],
        [VMEM],
        [pltpu.SemaphoreType.DMA((2, 2))],
    )(own)
    far0 = lax.ppermute(chunk0, "rows", far_route)
    kept_self, given_self, my_energy = call(
        "self",
        self_kernel,
        [(half_shape, f32), (half_shape, bf16), ((8, TS), f32)],
        [SMEM, SMEM, VMEM],
        [pltpu.VMEM((2, 2, HALF, TS), f32), pltpu.VMEM((TS, 128), f32)],
        after=after,
    )(pos, band_tiles, own)
    other_energy = lax.ppermute(my_energy, "freq", swap)
    got_self = lax.ppermute(given_self, "freq", swap)
    message = call("message", message_kernel, [((8, TS), f32)], [VMEM] * 2, flops=MCOST)(
        my_energy, other_energy
    )
    far1 = lax.ppermute(chunk1, "rows", far_route)
    near = lax.ppermute(own, "rows", pair)
    far = (far0, far1)
    near_message = lax.ppermute(message, "rows", pair)
    far_message = lax.ppermute(near_message, "rows", across_route)

    unit_shape = (2, 2, 2, CR, HALF)
    after = call("order", order_kernel, [token], [ANY], flops=TCOST)(far0)
    products = []
    for j in range(CHUNKS):
        kept, given = call(
            f"pair{j}",
            lambda *refs, j=j: pair_kernel(j, *refs),
            [(unit_shape, f32), (unit_shape, bf16)],
            [SMEM] * 4 + [VMEM] * 6,
            [pltpu.VMEM((TS, 128), f32)],
            flops=PCOST,
            after=after,
        )(pos, message, near_message, far_message, own, near, far[j], message, near_message, far_message)
        got = lax.ppermute(given, "freq", swap)
        if j == 0:
            after = call(
                "order1", order_kernel, [token], [ANY, ANY], flops=FCOST, after=kept
            )(got_self, far[1])
        products.append((kept, got))
    out, after = call(
        "finish",
        self_finish_kernel,
        [((2, 1, 3, HALF, TS), bf16), token],
        [SMEM] + [VMEM] * 4,
        [
            pltpu.VMEM((2, HALF, TS), bf16),
            pltpu.VMEM((2, TS, 128), f32),
            pltpu.SemaphoreType.DMA((2,)),
        ],
        after=kept,
        out_specs=[ANY, VMEM],
    )(pos, kept_self, got_self, my_energy, other_energy)
    for j, (kept, got) in enumerate(products):
        fin = call("decode", pair_finish_kernel, [(unit_shape, bf16)], [VMEM, VMEM], after=after)(kept, got)
        after = fin
        back = lax.ppermute(fin, "rows", back_route)
        out = call(
            f"place{j}",
            lambda *refs, j=j: place_kernel(j, *refs),
            [((2, 1, 3, HALF, TS), bf16)],
            [SMEM, ANY, VMEM, VMEM],
            [pltpu.SemaphoreType.DMA((16,))],
            out_specs=ANY,
            aliases={1: 0},
        )(pos, out, fin, back)
    return out


def solution(mesh):
    return jax.shard_map(
        shards,
        mesh=mesh,
        in_specs=(P(None, "rows", None, None, "freq"), P("rows", None)),
        out_specs=P(None, "rows", None, "freq", None),
        check_vma=False,
    )
```

```python
import jax
import jax.numpy as jnp
from jax import lax
from jax.experimental import pallas as pl
from jax.experimental.pallas import tpu as pltpu
from jax.sharding import PartitionSpec as P

TS = 512
HALF = 256
BAND = 4
CHUNKS = 2
CR = HALF // CHUNKS
TILES = 8
EPSILON = 1e-06
TINY = 1e-30
CODE = 2.0**7.5
VMEM = pl.BlockSpec(memory_space=pltpu.VMEM)
ANY = pl.BlockSpec(memory_space=pl.ANY)
SMEM = pl.BlockSpec(memory_space=pltpu.SMEM)
MIB = 1024 * 1024
MCOST = 0
PCOST = 0
TCOST = 2**32
FCOST = 2**33


def encode(x):
    u = x * CODE
    y = u * u
    y = y * y
    y = y * y
    y = y * y
    return jnp.where(u < 0, -y, y).astype(jnp.bfloat16)


def decode(y):
    y = y.astype(jnp.float32)
    r = lax.rsqrt(lax.rsqrt(lax.rsqrt(lax.rsqrt(jnp.abs(y))))) * (1.0 / CODE)
    return jnp.where(y < 0, -r, r)


def column(row):
    width = row.shape[1]
    return jnp.transpose(jnp.broadcast_to(row, (128, width)))


def tile_rows(unit, part, tile):
    return pl.ds(((unit * 2 + part) * 2 + tile) * CR, CR)


def put_energies(messages, given_ref):
    for i, message in enumerate(messages):
        rest = message[0:1, :]
        for level in range(3):
            term = rest.astype(jnp.bfloat16)
            rest = rest - term.astype(jnp.float32)
            for h in range(2):
                row = TILES * CR + (i * 3 + level) * 2 + h
                given_ref[row : row + 1, :] = term[:, h * HALF : h * HALF + HALF]


def get_energy(got_ref, i):
    tail = got_ref[TILES * CR :, :].astype(jnp.float32)
    halves = []
    for h in range(2):
        rows = [tail[(i * 3 + level) * 2 + h :][:1] for level in range(3)]
        halves.append(rows[0] + (rows[1] + rows[2]))
    return jnp.concatenate(halves, axis=1)


def inverse(energy):
    return lax.rsqrt(jnp.maximum(energy, TINY))


def chunk_of_lanes(row, j):
    return jnp.concatenate(
        [row[:, h * HALF + j * CR : h * HALF + j * CR + CR] for h in range(2)], axis=1
    )


def complex_product(left, right_re, right_im):
    dims = (((1,), (1,)), ((), ()))
    with_re = lax.dot_general(left, right_re, dims, preferred_element_type=jnp.float32)
    with_im = lax.dot_general(left, right_im, dims, preferred_element_type=jnp.float32)
    rows = left.shape[0] // 2
    return with_re[:rows] + with_im[rows:], with_re[rows:] - with_im[:rows]


def chunk_copies(j, own_ref, chunk_ref, sem):
    return [
        pltpu.make_async_copy(
            own_ref.at[:, :, pl.ds(half * HALF + j * CR, CR), :],
            chunk_ref.at[:, :, half],
            sem.at[half],
        )
        for half in range(2)
    ]


def run(copies):
    for copy in copies:
        copy.start()
    for copy in copies:
        copy.wait()


def pack_kernel(own_ref, chunk0_ref, token_ref, sem):
    token_ref[...] = jnp.zeros_like(token_ref)
    run(chunk_copies(0, own_ref, chunk0_ref, sem))


def order_kernel(*refs):
    token_ref = refs[-1]
    token_ref[...] = jnp.zeros_like(token_ref)


def second_kernel(own_ref, chunk1_ref, sem):
    run(chunk_copies(1, own_ref, chunk1_ref, sem))


def self_kernel(pos_ref, band_ref, own_ref, kept_ref, given_ref, msg_ref, product_ref, col_ref):
    mine = pos_ref[1]
    msg_ref[...] = jnp.zeros_like(msg_ref)
    for d in range(BAND):
        msg_ref[1 + d : 2 + d, :] = jnp.full((1, TS), band_ref[0, d].astype(jnp.float32))
    right_re = jnp.concatenate([own_ref[0, d] for d in range(BAND)], axis=1)
    right_im = jnp.concatenate([own_ref[1, d] for d in range(BAND)], axis=1)
    diagonal = lax.broadcasted_iota(jnp.int32, (HALF, HALF), 0) == lax.broadcasted_iota(
        jnp.int32, (HALF, HALF), 1
    )
    for half in range(2):
        start = half * HALF
        left = jnp.concatenate(
            [
                jnp.concatenate(
                    [own_ref[part, d, start : start + HALF, :] for d in range(BAND)], axis=1
                )
                for part in range(2)
            ],
            axis=0,
        )
        real, imag = complex_product(left, right_re, right_im)
        product_ref[half, 0] = real
        product_ref[half, 1] = imag
        energies = jnp.where(diagonal, real[:, start : start + HALF], 0.0)
        msg_ref[0:1, start : start + HALF] = jnp.sum(energies, axis=0, keepdims=True)
        col_ref[start : start + HALF, :] = jnp.broadcast_to(
            jnp.sum(energies, axis=1, keepdims=True), (HALF, 128)
        )
    other = pl.multiple_of((1 - mine) * HALF, HALF)
    scale = lax.rsqrt(jnp.maximum(col_ref[pl.ds(other, HALF), 0:1], TINY)) * lax.rsqrt(
        jnp.maximum(msg_ref[0:1, :], TINY)
    )
    for part in range(2):
        given_ref[part] = encode(product_ref[1 - mine, part] * scale)
        kept_ref[part] = product_ref[mine, part]


def pair_kernel(
    j, pos_ref, own_s, near_s, far_s, own_ref, near_ref, far_ref, own_m, near_m, far_m,
    kept_ref, given_ref, col_ref,
):
    core = pos_ref[0]
    mine = pos_ref[1]
    if j == 0:
        given_ref[TILES * CR :, :] = jnp.zeros((32, HALF), jnp.bfloat16)
        put_energies((own_m, near_m, far_m), given_ref)

    def shift(left_s, right_s):
        first = right_s[1, 0]
        return sum((left_s[1 + d, 0] < first).astype(jnp.int32) for d in range(BAND))

    def aligned(load, part, s):
        blocks = []
        for d in range(BAND):
            block = load(part, jnp.maximum(d - s, 0))
            if d < 2:
                block = jnp.where(d >= s, block, jnp.zeros_like(block))
            blocks.append(block)
        return jnp.concatenate(blocks, axis=1)

    def chunk_of_rows(ref):
        def load(part, k):
            return jnp.concatenate(
                [ref[part, k, h * HALF + j * CR : h * HALF + j * CR + CR, :] for h in range(2)],
                axis=0,
            )
        return load

    def emit(unit, keep, real, imag, start, rows, row, split):
        for part, value in enumerate((real, imag)):
            if not keep:
                value = encode(value * (col_ref[pl.ds(start, rows), 0:1] * row))
            for tile in range(2):
                piece = split(value, tile)
                if keep:
                    kept_ref[unit, part, tile] = piece
                else:
                    given_ref[tile_rows(unit, part, tile), :] = piece

    @pl.when(core == 0)
    def _():
        col_ref[...] = column(inverse(own_m[0:1, :]))
        units = (
            (near_s, chunk_of_rows(near_ref), near_m),
            (far_s, lambda part, k: far_ref[part, k].reshape(2 * CR, HALF), far_m),
        )
        for unit, (right_s, load, right_m) in enumerate(units):
            s = shift(own_s, right_s)
            right_re = aligned(load, 0, s)
            right_im = aligned(load, 1, s)
            row = inverse(chunk_of_lanes(right_m[0:1, :], j))
            for keep in (False, True):
                start = pl.multiple_of((mine if keep else 1 - mine) * HALF, HALF)
                left = jnp.concatenate(
                    [
                        jnp.concatenate(
                            [own_ref[part, d, pl.ds(start, HALF), :] for d in range(BAND)], axis=1
                        )
                        for part in range(2)
                    ],
                    axis=0,
                )
                real, imag = complex_product(left, right_re, right_im)
                emit(unit, keep, real, imag, start, HALF, row, lambda v, t: v[t * CR : t * CR + CR])

    @pl.when(core == 1)
    def _():
        col_ref[...] = column(inverse(far_m[0:1, :]))
        units = ((near_s, near_ref, near_m), (own_s, own_ref, own_m))
        for unit, (right_s, right_ref, right_m) in enumerate(units):
            s = shift(far_s, right_s)
            load = lambda part, k: right_ref[part, k]
            right_re = aligned(load, 0, s)
            right_im = aligned(load, 1, s)
            row = inverse(right_m[0:1, :])
            for keep in (False, True):
                half = mine if keep else 1 - mine
                left = jnp.concatenate(
                    [
                        jnp.concatenate([far_ref[part, d, half] for d in range(BAND)], axis=1)
                        for part in range(2)
                    ],
                    axis=0,
                )
                real, imag = complex_product(left, right_re, right_im)
                start = pl.multiple_of(half * HALF + j * CR, CR)
                emit(unit, keep, real, imag, start, CR, row, lambda v, t: v[:, t * HALF : t * HALF + HALF])


def self_finish_kernel(
    pos_ref, kept_ref, got_ref, mine_ref, first_ref, out_ref, token_ref, fin_ref, col_ref, sem
):
    token_ref[...] = jnp.zeros_like(token_ref)
    start = pl.multiple_of(pos_ref[1] * HALF, HALF)
    energy = get_energy(first_ref, 0)
    other = jnp.sqrt(jnp.maximum(energy, TINY))
    total = mine_ref[0:1, :] + energy
    col_ref[0] = column(other)
    col_ref[1] = column(total)
    scale = lax.rsqrt(col_ref[1, pl.ds(start, HALF), 0:1] * total + EPSILON)
    back = col_ref[0, pl.ds(start, HALF), 0:1] * other
    for part in range(2):
        value = (kept_ref[part] + decode(got_ref[part]) * back) * scale
        fin_ref[part] = value.astype(jnp.bfloat16)
    copies = [
        pltpu.make_async_copy(fin_ref.at[part], out_ref.at[part, 0, 0], sem.at[part])
        for part in range(2)
    ]
    for copy in copies:
        copy.start()
    for copy in copies:
        copy.wait()


def pair_finish_kernel(
    j, pos_ref, kept_ref, got_ref, own_m, near_m, far_m, first_ref, fin_ref, col_ref
):
    core = pos_ref[0]
    mine = pos_ref[1]
    other = [get_energy(first_ref, i) for i in range(3)]
    total = [m[0:1, :] + o for m, o in zip((own_m, near_m, far_m), other)]
    root = [jnp.sqrt(jnp.maximum(o, TINY)) for o in other]

    def emit(unit, tile, start, root_row, total_row):
        back = col_ref[0, pl.ds(start, CR), 0:1] * root_row
        scale = lax.rsqrt(col_ref[1, pl.ds(start, CR), 0:1] * total_row + EPSILON)
        for part in range(2):
            value = kept_ref[unit, part, tile] + decode(got_ref[tile_rows(unit, part, tile), :]) * back
            fin_ref[unit, part, tile] = (value * scale).astype(jnp.bfloat16)

    @pl.when(core == 0)
    def _():
        col_ref[0] = column(root[0])
        col_ref[1] = column(total[0])
        for unit, i in enumerate((1, 2)):
            for tile in range(2):
                start = pl.multiple_of(mine * HALF + tile * CR, CR)
                emit(unit, tile, start, chunk_of_lanes(root[i], j), chunk_of_lanes(total[i], j))

    @pl.when(core == 1)
    def _():
        col_ref[0] = column(root[2])
        col_ref[1] = column(total[2])
        start = pl.multiple_of(mine * HALF + j * CR, CR)
        for unit, i in enumerate((1, 0)):
            for tile in range(2):
                lanes = slice(tile * HALF, tile * HALF + HALF)
                emit(unit, tile, start, root[i][:, lanes], total[i][:, lanes])


def place_kernel(j, pos_ref, out_in_ref, fin_ref, back_ref, out_ref, sem):
    del out_in_ref
    rows = pl.ds(j * CR, CR)
    pieces = [(unit, part, tile) for unit in range(2) for part in range(2) for tile in range(2)]

    @pl.when(pos_ref[0] == 0)
    def _():
        run(
            [
                pltpu.make_async_copy(
                    fin_ref.at[unit, part, tile, :, pl.ds(h * CR, CR)],
                    out_ref.at[
                        part, 0, 1 + unit, pl.ds(tile * CR, CR), pl.ds(h * HALF + j * CR, CR)
                    ],
                    sem.at[2 * i + h],
                )
                for i, (unit, part, tile) in enumerate(pieces)
                for h in range(2)
            ]
        )

    @pl.when(pos_ref[0] == 1)
    def _():
        run(
            [
                pltpu.make_async_copy(
                    back_ref.at[unit, part, tile],
                    out_ref.at[part, 0, 1 + unit, rows, pl.ds(tile * HALF, HALF)],
                    sem.at[i],
                )
                for i, (unit, part, tile) in enumerate(pieces)
            ]
        )


def call(name, kernel, outs, specs, scratch=(), flops=0, after=None, out_specs=None, aliases=None, vmem=40):
    shapes = [jax.ShapeDtypeStruct(shape, dtype) for shape, dtype in outs]
    body = kernel if after is None else lambda _, *refs: kernel(*refs)
    run = pl.pallas_call(
        body,
        name=name,
        out_shape=shapes if len(shapes) > 1 else shapes[0],
        in_specs=specs if after is None else [ANY, *specs],
        out_specs=out_specs or ([VMEM] * len(shapes) if len(shapes) > 1 else VMEM),
        scratch_shapes=list(scratch),
        compiler_params=pltpu.CompilerParams(vmem_limit_bytes=vmem * MIB),
        input_output_aliases=aliases or {},
        cost_estimate=pl.CostEstimate(flops=flops, bytes_accessed=2**21, transcendentals=0),
    )
    return run if after is None else lambda *args: run(after, *args)


def shards(correlation, band_tiles):
    bf16, f32 = jnp.bfloat16, jnp.float32
    count = lax.axis_size("rows")
    core = lax.axis_index("rows") % 2
    mine = lax.axis_index("freq") % 2
    pos = jnp.stack([core, mine]).astype(jnp.int32)
    own = correlation.reshape(2, BAND, TS, HALF)
    swap = [(i, i ^ 1) for i in range(lax.axis_size("freq"))]
    pair = [(i, i ^ 1) for i in range(count)]
    far_route = [(i + 2, i) for i in range(0, count - 2, 2)] + [(i - 2, i) for i in range(3, count, 2)]
    across_route = [(i + 3, i) for i in range(0, count - 2, 2)] + [(i - 3, i) for i in range(3, count, 2)]
    back_route = [(i, i - 2) for i in range(3, count, 2)]

    chunk_shape = (2, BAND, 2, CR, HALF)
    half_shape = (2, HALF, TS)
    token = ((8, 128), f32)
    chunk0, after = call(
        "pack",
        pack_kernel,
        [(chunk_shape, bf16), token],
        [ANY],
        [pltpu.SemaphoreType.DMA((2,))],
        vmem=52,
    )(own)
    far0 = lax.ppermute(chunk0, "rows", far_route)
    kept_self, given_self, message = call(
        "self",
        self_kernel,
        [(half_shape, f32), (half_shape, bf16), ((8, TS), f32)],
        [SMEM, SMEM, VMEM],
        [pltpu.VMEM((2, 2, HALF, TS), f32), pltpu.VMEM((TS, 128), f32)],
        after=after,
    )(pos, band_tiles, own)
    got_self = lax.ppermute(given_self, "freq", swap)
    near_message = lax.ppermute(message, "rows", pair)
    far_message = lax.ppermute(near_message, "rows", across_route)
    chunk1 = call(
        "second",
        second_kernel,
        [(chunk_shape, bf16)],
        [VMEM],
        [pltpu.SemaphoreType.DMA((2,))],
        after=given_self,
    )(own)
    far1 = lax.ppermute(chunk1, "rows", far_route)
    near = lax.ppermute(own, "rows", pair)
    far = (far0, far1)

    unit_shape = (2, 2, 2, CR, HALF)
    after = call("order", order_kernel, [token], [ANY], flops=TCOST)(far0)
    products = []
    for j in range(CHUNKS):
        kept, given = call(
            f"pair{j}",
            lambda *refs, j=j: pair_kernel(j, *refs),
            [(unit_shape, f32), (((TILES * CR + (32 if j == 0 else 0)), HALF), bf16)],
            [SMEM] * 4 + [VMEM] * 6,
            [pltpu.VMEM((TS, 128), f32)],
            flops=PCOST,
            after=after,
        )(pos, message, near_message, far_message, own, near, far[j], message, near_message, far_message)
        got = lax.ppermute(given, "freq", swap)
        if j == 0:
            after = call(
                "order1", order_kernel, [token], [ANY], flops=FCOST, after=kept
            )(got_self)
        products.append((kept, got))
    for j, (kept, got) in enumerate(products):
        fin = call(
            f"decode{j}",
            lambda *refs, j=j: pair_finish_kernel(j, *refs),
            [(unit_shape, bf16)],
            [SMEM] + [VMEM] * 6,
            [pltpu.VMEM((2, TS, 128), f32)],
            after=after,
        )(pos, kept, got, message, near_message, far_message, products[0][1])
        back = lax.ppermute(fin, "rows", back_route)
        if j == 0:
            out, after = call(
                "finish",
                self_finish_kernel,
                [((2, 1, 3, HALF, TS), bf16), token],
                [SMEM] + [VMEM] * 4,
                [
                    pltpu.VMEM((2, HALF, TS), bf16),
                    pltpu.VMEM((2, TS, 128), f32),
                    pltpu.SemaphoreType.DMA((2,)),
                ],
                after=fin,
                out_specs=[ANY, VMEM],
            )(pos, kept_self, got_self, message, products[0][1])
        out = call(
            f"place{j}",
            lambda *refs, j=j: place_kernel(j, *refs),
            [((2, 1, 3, HALF, TS), bf16)],
            [SMEM, ANY, VMEM, VMEM],
            [pltpu.SemaphoreType.DMA((16,))],
            out_specs=ANY,
            aliases={1: 0},
        )(pos, out, fin, back)
    return out


def solution(mesh):
    return jax.shard_map(
        shards,
        mesh=mesh,
        in_specs=(P(None, "rows", None, None, "freq"), P("rows", None)),
        out_specs=P(None, "rows", None, "freq", None),
        check_vma=False,
    )
```

```python
import jax
import jax.numpy as jnp
from jax import lax
from jax.experimental import pallas as pl
from jax.experimental.pallas import tpu as pltpu
from jax.sharding import PartitionSpec as P

TS = 512
HALF = 256
BAND = 4
CHUNKS = 2
CR = HALF // CHUNKS
TILES = 8
ROWS = 2 * BAND * 2 * CR
EPSILON = 1e-06
TINY = 1e-30
CODE = 2.0**7.5
VMEM = pl.BlockSpec(memory_space=pltpu.VMEM)
ANY = pl.BlockSpec(memory_space=pl.ANY)
SMEM = pl.BlockSpec(memory_space=pltpu.SMEM)
MIB = 1024 * 1024
MCOST = 0
PCOST = 0
TCOST = 2**32
FCOST = 2**33


def encode(x):
    u = x * CODE
    y = u * u
    y = y * y
    y = y * y
    y = y * y
    return jnp.where(u < 0, -y, y).astype(jnp.bfloat16)


def decode(y):
    y = y.astype(jnp.float32)
    r = lax.rsqrt(lax.rsqrt(lax.rsqrt(lax.rsqrt(jnp.abs(y))))) * (1.0 / CODE)
    return jnp.where(y < 0, -r, r)


def column(row):
    width = row.shape[1]
    return jnp.transpose(jnp.broadcast_to(row, (128, width)))


def tile_rows(unit, part, tile):
    return pl.ds(((unit * 2 + part) * 2 + tile) * CR, CR)


def put_energies(messages, given_ref):
    for i, message in enumerate(messages):
        rest = message
        for level in range(3):
            term = rest.astype(jnp.bfloat16)
            rest = rest - term.astype(jnp.float32)
            for h in range(2):
                row = TILES * CR + (i * 3 + level) * 2 + h
                given_ref[row : row + 1, :] = term[:, h * HALF : h * HALF + HALF]


def get_energy(got_ref, i):
    tail = got_ref[TILES * CR :, :].astype(jnp.float32)
    halves = []
    for h in range(2):
        rows = [tail[(i * 3 + level) * 2 + h :][:1] for level in range(3)]
        halves.append(rows[0] + (rows[1] + rows[2]))
    return jnp.concatenate(halves, axis=1)


def inverse(energy):
    return lax.rsqrt(jnp.maximum(energy, TINY))


def chunk_of_lanes(row, j):
    return jnp.concatenate(
        [row[:, h * HALF + j * CR : h * HALF + j * CR + CR] for h in range(2)], axis=1
    )


def complex_product(left, right_re, right_im):
    dims = (((1,), (1,)), ((), ()))
    with_re = lax.dot_general(left, right_re, dims, preferred_element_type=jnp.float32)
    with_im = lax.dot_general(left, right_im, dims, preferred_element_type=jnp.float32)
    rows = left.shape[0] // 2
    return with_re[:rows] + with_im[rows:], with_re[rows:] - with_im[:rows]


def live_before(band_ref, tile):
    return sum((band_ref[0, d] < tile).astype(jnp.int32) for d in range(BAND))


def run(copies):
    for copy in copies:
        copy.start()
    for copy in copies:
        copy.wait()


def pack_kernel(pos_ref, tiles_ref, own_ref, chunk0_ref, token_ref, shift_ref, band_ref, sem):
    bands = pltpu.make_async_copy(tiles_ref, band_ref, sem.at[17])
    bands.start()
    copies = [
        pltpu.make_async_copy(
            own_ref.at[part, d, pl.ds(half * HALF, CR), :],
            chunk0_ref.at[pl.ds(((part * BAND + d) * 2 + half) * CR, CR), :],
            sem.at[(part * BAND + d) * 2 + half],
        )
        for part in range(2)
        for d in range(BAND)
        for half in range(2)
    ]
    for copy in copies:
        copy.start()
    token_ref[...] = jnp.zeros_like(token_ref)
    shift_ref[...] = jnp.zeros_like(shift_ref)
    bands.wait()
    for offset in (1, 2):
        count = live_before(band_ref, pos_ref[2] + offset).astype(jnp.float32)
        shift_ref[offset : offset + 1, :] = jnp.full((1, HALF), count).astype(jnp.bfloat16)
    run([pltpu.make_async_copy(shift_ref, chunk0_ref.at[pl.ds(ROWS, 16), :], sem.at[16])])
    for copy in copies:
        copy.wait()


def order_kernel(*refs):
    token_ref = refs[-1]
    token_ref[...] = jnp.zeros_like(token_ref)


def second_kernel(own_ref, chunk1_ref, sem):
    run(
        [
            pltpu.make_async_copy(
                own_ref.at[part, d, pl.ds(half * HALF + CR, CR), :],
                chunk1_ref.at[pl.ds(((part * BAND + d) * 2 + half) * CR, CR), :],
                sem.at[(part * BAND + d) * 2 + half],
            )
            for part in range(2)
            for d in range(BAND)
            for half in range(2)
        ]
    )


def self_kernel(pos_ref, own_ref, kept_ref, given_ref, msg_ref, product_ref, col_ref):
    mine = pos_ref[1]
    msg_ref[...] = jnp.zeros_like(msg_ref)
    right_re = jnp.concatenate([own_ref[0, d] for d in range(BAND)], axis=1)
    right_im = jnp.concatenate([own_ref[1, d] for d in range(BAND)], axis=1)
    diagonal = lax.broadcasted_iota(jnp.int32, (HALF, HALF), 0) == lax.broadcasted_iota(
        jnp.int32, (HALF, HALF), 1
    )
    for half in range(2):
        start = half * HALF
        left = jnp.concatenate(
            [
                jnp.concatenate(
                    [own_ref[part, d, start : start + HALF, :] for d in range(BAND)], axis=1
                )
                for part in range(2)
            ],
            axis=0,
        )
        real, imag = complex_product(left, right_re, right_im)
        product_ref[half, 0] = real
        product_ref[half, 1] = imag
        energies = jnp.where(diagonal, real[:, start : start + HALF], 0.0)
        msg_ref[0:1, start : start + HALF] = jnp.sum(energies, axis=0, keepdims=True)
        col_ref[start : start + HALF, :] = jnp.broadcast_to(
            jnp.sum(energies, axis=1, keepdims=True), (HALF, 128)
        )
    other = pl.multiple_of((1 - mine) * HALF, HALF)
    scale = lax.rsqrt(jnp.maximum(col_ref[pl.ds(other, HALF), 0:1], TINY)) * lax.rsqrt(
        jnp.maximum(msg_ref[0:1, :], TINY)
    )
    for part in range(2):
        given_ref[part] = encode(product_ref[1 - mine, part] * scale)
        kept_ref[part] = product_ref[mine, part]


def row_energies(load, blocks):
    rows = []
    for block in range(blocks):
        total = jnp.zeros((CR, HALF), jnp.float32)
        for part in range(2):
            for d in range(BAND):
                wide = load(part, d, block).astype(jnp.float32)
                total += wide * wide
        folded = jnp.transpose(total[:, :128] + total[:, 128:])
        rows.append(jnp.sum(folded, axis=0, keepdims=True))
    return jnp.concatenate(rows, axis=1)


def pair_kernel(
    j, pos_ref, band_ref, own_ref, near_ref, far_ref, shift_ref, own_m, *rest
):
    if j == 0:
        kept_ref, given_ref, pair_m, col_ref = rest
    else:
        first_m, kept_ref, given_ref, pair_m, col_ref = rest
    core = pos_ref[0]
    mine = pos_ref[1]

    def far_block(part, k, half):
        start = pl.multiple_of(((part * BAND + k) * 2 + half) * CR, CR)
        return far_ref[pl.ds(start, CR), :]

    def far_chunk(part, k):
        start = pl.multiple_of((part * BAND + k) * 2 * CR, 2 * CR)
        return far_ref[pl.ds(start, 2 * CR), :]

    pair_m[...] = jnp.zeros_like(pair_m)
    if j == 0:
        pair_m[0:1, :] = row_energies(
            lambda part, d, block: near_ref[part, d, block * CR : block * CR + CR, :], TS // CR
        )
    else:
        pair_m[0:1, :] = first_m[0:1, :]
    pair_m[1:2, : 2 * CR] = row_energies(far_block, 2)
    near_row = pair_m[0:1, :]
    far_row = pair_m[1:2, : 2 * CR]
    given_ref[TILES * CR :, :] = jnp.zeros((32, HALF), jnp.bfloat16)
    put_energies((own_m[0:1, :], near_row, pair_m[1:2, :]), given_ref)

    def aligned(load, part, s):
        blocks = []
        for d in range(BAND):
            block = load(part, jnp.maximum(d - s, 0))
            if d < 2:
                block = jnp.where(d >= s, block, jnp.zeros_like(block))
            blocks.append(block)
        return jnp.concatenate(blocks, axis=1)

    def chunk_of_rows(ref):
        def load(part, k):
            return jnp.concatenate(
                [ref[part, k, h * HALF + j * CR : h * HALF + j * CR + CR, :] for h in range(2)],
                axis=0,
            )
        return load

    def emit(unit, keep, real, imag, start, rows, row, split):
        for part, value in enumerate((real, imag)):
            if not keep:
                value = encode(value * (col_ref[pl.ds(start, rows), 0:1] * row))
            for tile in range(2):
                piece = split(value, tile)
                if keep:
                    kept_ref[unit, part, tile] = piece
                else:
                    given_ref[tile_rows(unit, part, tile), :] = piece

    @pl.when(core == 0)
    def _():
        col_ref[...] = column(inverse(own_m[0:1, :]))
        units = (
            (chunk_of_rows(near_ref), chunk_of_lanes(near_row, j)),
            (far_chunk, far_row),
        )
        for unit, (load, energy) in enumerate(units):
            s = live_before(band_ref, pos_ref[2] + 1 + unit)
            right_re = aligned(load, 0, s)
            right_im = aligned(load, 1, s)
            row = inverse(energy)
            for keep in (False, True):
                start = pl.multiple_of((mine if keep else 1 - mine) * HALF, HALF)
                left = jnp.concatenate(
                    [
                        jnp.concatenate(
                            [own_ref[part, d, pl.ds(start, HALF), :] for d in range(BAND)], axis=1
                        )
                        for part in range(2)
                    ],
                    axis=0,
                )
                real, imag = complex_product(left, right_re, right_im)
                emit(unit, keep, real, imag, start, HALF, row, lambda v, t: v[t * CR : t * CR + CR])

    @pl.when(core == 1)
    def _():
        col_ref[: 2 * CR, :] = column(inverse(far_row))
        shifts = shift_ref[ROWS:, :].astype(jnp.float32)
        units = ((near_ref, near_row), (own_ref, own_m[0:1, :]))
        for unit, (right_ref, energy) in enumerate(units):
            s = jnp.max(shifts[unit + 1 : unit + 2, :]).astype(jnp.int32)
            load = lambda part, k: right_ref[part, k]
            right_re = aligned(load, 0, s)
            right_im = aligned(load, 1, s)
            row = inverse(energy)
            for keep in (False, True):
                half = mine if keep else 1 - mine
                left = jnp.concatenate(
                    [
                        jnp.concatenate([far_block(part, d, half) for d in range(BAND)], axis=1)
                        for part in range(2)
                    ],
                    axis=0,
                )
                real, imag = complex_product(left, right_re, right_im)
                start = pl.multiple_of(half * CR, CR)
                emit(unit, keep, real, imag, start, CR, row, lambda v, t: v[:, t * HALF : t * HALF + HALF])


def self_finish_kernel(
    pos_ref, kept_ref, got_ref, mine_ref, first_ref, out_ref, token_ref, fin_ref, col_ref, sem
):
    token_ref[...] = jnp.zeros_like(token_ref)
    start = pl.multiple_of(pos_ref[1] * HALF, HALF)
    energy = get_energy(first_ref, 0)
    other = jnp.sqrt(jnp.maximum(energy, TINY))
    total = mine_ref[0:1, :] + energy
    col_ref[0] = column(other)
    col_ref[1] = column(total)
    scale = lax.rsqrt(col_ref[1, pl.ds(start, HALF), 0:1] * total + EPSILON)
    back = col_ref[0, pl.ds(start, HALF), 0:1] * other
    for part in range(2):
        value = (kept_ref[part] + decode(got_ref[part]) * back) * scale
        fin_ref[part] = value.astype(jnp.bfloat16)
    copies = [
        pltpu.make_async_copy(fin_ref.at[part], out_ref.at[part, 0, 0], sem.at[part])
        for part in range(2)
    ]
    for copy in copies:
        copy.start()
    for copy in copies:
        copy.wait()


def pair_finish_kernel(j, pos_ref, kept_ref, got_ref, own_m, pair_m, fin_ref, col_ref):
    core = pos_ref[0]
    mine = pos_ref[1]
    other = [get_energy(got_ref, i) for i in range(3)]
    total = [m + o for m, o in zip((own_m[0:1, :], pair_m[0:1, :], pair_m[1:2, :]), other)]
    root = [jnp.sqrt(jnp.maximum(o, TINY)) for o in other]

    def emit(unit, tile, start, root_row, total_row):
        back = col_ref[0, pl.ds(start, CR), 0:1] * root_row
        scale = lax.rsqrt(col_ref[1, pl.ds(start, CR), 0:1] * total_row + EPSILON)
        for part in range(2):
            value = kept_ref[unit, part, tile] + decode(got_ref[tile_rows(unit, part, tile), :]) * back
            fin_ref[unit, part, tile] = (value * scale).astype(jnp.bfloat16)

    @pl.when(core == 0)
    def _():
        col_ref[0] = column(root[0])
        col_ref[1] = column(total[0])
        for tile in range(2):
            start = pl.multiple_of(mine * HALF + tile * CR, CR)
            emit(0, tile, start, chunk_of_lanes(root[1], j), chunk_of_lanes(total[1], j))
            emit(1, tile, start, root[2][:, : 2 * CR], total[2][:, : 2 * CR])

    @pl.when(core == 1)
    def _():
        col_ref[0] = column(root[2])
        col_ref[1] = column(total[2])
        start = pl.multiple_of(mine * CR, CR)
        for unit, i in enumerate((1, 0)):
            for tile in range(2):
                lanes = slice(tile * HALF, tile * HALF + HALF)
                emit(unit, tile, start, root[i][:, lanes], total[i][:, lanes])


def place_kernel(j, pos_ref, out_in_ref, fin_ref, back_ref, out_ref, sem):
    del out_in_ref
    rows = pl.ds(j * CR, CR)
    pieces = [(unit, part, tile) for unit in range(2) for part in range(2) for tile in range(2)]

    @pl.when(pos_ref[0] == 0)
    def _():
        run(
            [
                pltpu.make_async_copy(
                    fin_ref.at[unit, part, tile, :, pl.ds(h * CR, CR)],
                    out_ref.at[
                        part, 0, 1 + unit, pl.ds(tile * CR, CR), pl.ds(h * HALF + j * CR, CR)
                    ],
                    sem.at[2 * i + h],
                )
                for i, (unit, part, tile) in enumerate(pieces)
                for h in range(2)
            ]
        )

    @pl.when(pos_ref[0] == 1)
    def _():
        run(
            [
                pltpu.make_async_copy(
                    back_ref.at[unit, part, tile],
                    out_ref.at[part, 0, 1 + unit, rows, pl.ds(tile * HALF, HALF)],
                    sem.at[i],
                )
                for i, (unit, part, tile) in enumerate(pieces)
            ]
        )


def call(name, kernel, outs, specs, scratch=(), flops=0, after=None, out_specs=None, aliases=None, vmem=40):
    shapes = [jax.ShapeDtypeStruct(shape, dtype) for shape, dtype in outs]
    body = kernel if after is None else lambda _, *refs: kernel(*refs)
    run = pl.pallas_call(
        body,
        name=name,
        out_shape=shapes if len(shapes) > 1 else shapes[0],
        in_specs=specs if after is None else [ANY, *specs],
        out_specs=out_specs or ([VMEM] * len(shapes) if len(shapes) > 1 else VMEM),
        scratch_shapes=list(scratch),
        compiler_params=pltpu.CompilerParams(vmem_limit_bytes=vmem * MIB),
        input_output_aliases=aliases or {},
        cost_estimate=pl.CostEstimate(flops=flops, bytes_accessed=2**21, transcendentals=0),
    )
    return run if after is None else lambda *args: run(after, *args)


def shards(correlation, band_tiles):
    bf16, f32 = jnp.bfloat16, jnp.float32
    count = lax.axis_size("rows")
    core = lax.axis_index("rows") % 2
    mine = lax.axis_index("freq") % 2
    pos = jnp.stack([core, mine, lax.axis_index("rows")]).astype(jnp.int32)
    own = correlation.reshape(2, BAND, TS, HALF)
    swap = [(i, i ^ 1) for i in range(lax.axis_size("freq"))]
    pair = [(i, i ^ 1) for i in range(count)]
    far_route = [(i + 2, i) for i in range(0, count - 2, 2)] + [(i - 2, i) for i in range(3, count, 2)]
    back_route = [(i, i - 2) for i in range(3, count, 2)]

    half_shape = (2, HALF, TS)
    token = ((8, 128), f32)
    chunk0, after = call(
        "pack",
        pack_kernel,
        [((ROWS + 16, HALF), bf16), token],
        [SMEM, ANY, ANY],
        [pltpu.VMEM((16, HALF), bf16), pltpu.SMEM((1, BAND), jnp.int32), pltpu.SemaphoreType.DMA((18,))],
        vmem=52,
    )(pos, band_tiles, own)
    far0 = lax.ppermute(chunk0, "rows", far_route)
    kept_self, given_self, message = call(
        "self",
        self_kernel,
        [(half_shape, f32), (half_shape, bf16), ((8, TS), f32)],
        [SMEM, VMEM],
        [pltpu.VMEM((2, 2, HALF, TS), f32), pltpu.VMEM((TS, 128), f32)],
        after=after,
    )(pos, own)
    got_self = lax.ppermute(given_self, "freq", swap)
    chunk1 = call(
        "second",
        second_kernel,
        [((ROWS, HALF), bf16)],
        [VMEM],
        [pltpu.SemaphoreType.DMA((16,))],
        after=given_self,
    )(own)
    far1 = lax.ppermute(chunk1, "rows", far_route)
    near = lax.ppermute(own, "rows", pair)
    far = (far0, far1)

    unit_shape = (2, 2, 2, CR, HALF)
    after = call("order", order_kernel, [token], [ANY], flops=TCOST)(far0)
    products, pairs = [], []
    for j in range(CHUNKS):
        kept, given, pair_m = call(
            f"pair{j}",
            lambda *refs, j=j: pair_kernel(j, *refs),
            [(unit_shape, f32), ((TILES * CR + 32, HALF), bf16), ((8, TS), f32)],
            [SMEM, SMEM] + [VMEM] * (5 + j),
            [pltpu.VMEM((TS, 128), f32)],
            flops=PCOST,
            after=after,
        )(pos, band_tiles, own, near, far[j], far0, message, *pairs)
        pairs.append(pair_m)
        got = lax.ppermute(given, "freq", swap)
        if j == 0:
            after = call(
                "order1", order_kernel, [token], [ANY], flops=FCOST, after=kept
            )(got_self)
        products.append((kept, got))
    for j, (kept, got) in enumerate(products):
        fin = call(
            f"decode{j}",
            lambda *refs, j=j: pair_finish_kernel(j, *refs),
            [(unit_shape, bf16)],
            [SMEM] + [VMEM] * 4,
            [pltpu.VMEM((2, TS, 128), f32)],
            after=after,
        )(pos, kept, got, message, pairs[j])
        back = lax.ppermute(fin, "rows", back_route)
        if j == 0:
            out, after = call(
                "finish",
                self_finish_kernel,
                [((2, 1, 3, HALF, TS), bf16), token],
                [SMEM] + [VMEM] * 4,
                [
                    pltpu.VMEM((2, HALF, TS), bf16),
                    pltpu.VMEM((2, TS, 128), f32),
                    pltpu.SemaphoreType.DMA((2,)),
                ],
                after=fin,
                out_specs=[ANY, VMEM],
            )(pos, kept_self, got_self, message, products[0][1])
        out = call(
            f"place{j}",
            lambda *refs, j=j: place_kernel(j, *refs),
            [((2, 1, 3, HALF, TS), bf16)],
            [SMEM, ANY, VMEM, VMEM],
            [pltpu.SemaphoreType.DMA((16,))],
            out_specs=ANY,
            aliases={1: 0},
        )(pos, out, fin, back)
    return out


def solution(mesh):
    return jax.shard_map(
        shards,
        mesh=mesh,
        in_specs=(P(None, "rows", None, None, "freq"), P("rows", None)),
        out_specs=P(None, "rows", None, "freq", None),
        check_vma=False,
    )
```

```python
import jax
import jax.numpy as jnp
from jax import lax
from jax.experimental import pallas as pl
from jax.experimental.pallas import tpu as pltpu
from jax.sharding import PartitionSpec as P

TS = 512
HALF = 256
BAND = 4
CHUNKS = 2
CR = HALF // CHUNKS
TILES = 4
ROWS = 2 * BAND * 2 * CR
EPSILON = 1e-06
TINY = 1e-30
CODE = 2.0**7.5
VMEM = pl.BlockSpec(memory_space=pltpu.VMEM)
ANY = pl.BlockSpec(memory_space=pl.ANY)
SMEM = pl.BlockSpec(memory_space=pltpu.SMEM)
MIB = 1024 * 1024
PCOST = 0
TCOST = 2**32
FCOST = 2**35


def encode(x):
    u = x * CODE
    y = u * u
    y = y * y
    y = y * y
    y = y * y
    return jnp.where(u < 0, -y, y).astype(jnp.bfloat16)


def decode(y):
    y = y.astype(jnp.float32)
    r = lax.rsqrt(lax.rsqrt(lax.rsqrt(lax.rsqrt(jnp.abs(y))))) * (1.0 / CODE)
    return jnp.where(y < 0, -r, r)


def column(row):
    width = row.shape[1]
    return jnp.transpose(jnp.broadcast_to(row, (128, width)))


def tile_rows(part, tile):
    return pl.ds((part * 2 + tile) * CR, CR)


def put_energies(messages, given_ref):
    for i, message in enumerate(messages):
        rest = message
        for level in range(3):
            term = rest.astype(jnp.bfloat16)
            rest = rest - term.astype(jnp.float32)
            for h in range(2):
                row = TILES * CR + (i * 3 + level) * 2 + h
                given_ref[row : row + 1, :] = term[:, h * HALF : h * HALF + HALF]


def get_energy(got_ref, i):
    tail = got_ref[TILES * CR :, :].astype(jnp.float32)
    halves = []
    for h in range(2):
        rows = [tail[(i * 3 + level) * 2 + h :][:1] for level in range(3)]
        halves.append(rows[0] + (rows[1] + rows[2]))
    return jnp.concatenate(halves, axis=1)


def inverse(energy):
    return lax.rsqrt(jnp.maximum(energy, TINY))


def chunk_of_lanes(row, j):
    return jnp.concatenate(
        [row[:, h * HALF + j * CR : h * HALF + j * CR + CR] for h in range(2)], axis=1
    )


def complex_product(left, right_re, right_im):
    dims = (((1,), (1,)), ((), ()))
    with_re = lax.dot_general(left, right_re, dims, preferred_element_type=jnp.float32)
    with_im = lax.dot_general(left, right_im, dims, preferred_element_type=jnp.float32)
    rows = left.shape[0] // 2
    return with_re[:rows] + with_im[rows:], with_re[rows:] - with_im[:rows]


def live_before(band_ref, tile):
    return sum((band_ref[0, d] < tile).astype(jnp.int32) for d in range(BAND))


def run(copies):
    for copy in copies:
        copy.start()
    for copy in copies:
        copy.wait()


def pack_kernel(pos_ref, tiles_ref, own_ref, chunk0_ref, token_ref, shift_ref, band_ref, sem):
    bands = pltpu.make_async_copy(tiles_ref, band_ref, sem.at[17])
    bands.start()
    copies = [
        pltpu.make_async_copy(
            own_ref.at[part, d, pl.ds(half * HALF, CR), :],
            chunk0_ref.at[pl.ds(((part * BAND + d) * 2 + half) * CR, CR), :],
            sem.at[(part * BAND + d) * 2 + half],
        )
        for part in range(2)
        for d in range(BAND)
        for half in range(2)
    ]
    for copy in copies:
        copy.start()
    token_ref[...] = jnp.zeros_like(token_ref)
    shift_ref[...] = jnp.zeros_like(shift_ref)
    bands.wait()
    for offset in (1, 2):
        count = live_before(band_ref, pos_ref[2] + offset).astype(jnp.float32)
        shift_ref[offset : offset + 1, :] = jnp.full((1, HALF), count).astype(jnp.bfloat16)
    run([pltpu.make_async_copy(shift_ref, chunk0_ref.at[pl.ds(ROWS, 16), :], sem.at[16])])
    for copy in copies:
        copy.wait()


def order_kernel(*refs):
    token_ref = refs[-1]
    token_ref[...] = jnp.zeros_like(token_ref)


def second_kernel(own_ref, chunk1_ref, sem):
    run(
        [
            pltpu.make_async_copy(
                own_ref.at[part, d, pl.ds(half * HALF + CR, CR), :],
                chunk1_ref.at[pl.ds(((part * BAND + d) * 2 + half) * CR, CR), :],
                sem.at[(part * BAND + d) * 2 + half],
            )
            for part in range(2)
            for d in range(BAND)
            for half in range(2)
        ]
    )


def self_kernel(
    pos_ref, own_ref, kept_ref, given_ref, msg_ref, again_ref, product_ref, col_ref, sem
):
    mine = pos_ref[1]
    again = pltpu.make_async_copy(own_ref, again_ref, sem)
    again.start()
    msg_ref[...] = jnp.zeros_like(msg_ref)
    right_re = jnp.concatenate([own_ref[0, d] for d in range(BAND)], axis=1)
    right_im = jnp.concatenate([own_ref[1, d] for d in range(BAND)], axis=1)
    diagonal = lax.broadcasted_iota(jnp.int32, (HALF, HALF), 0) == lax.broadcasted_iota(
        jnp.int32, (HALF, HALF), 1
    )
    for half in range(2):
        start = half * HALF
        left = jnp.concatenate(
            [
                jnp.concatenate(
                    [own_ref[part, d, start : start + HALF, :] for d in range(BAND)], axis=1
                )
                for part in range(2)
            ],
            axis=0,
        )
        real, imag = complex_product(left, right_re, right_im)
        product_ref[half, 0] = real
        product_ref[half, 1] = imag
        energies = jnp.where(diagonal, real[:, start : start + HALF], 0.0)
        msg_ref[0:1, start : start + HALF] = jnp.sum(energies, axis=0, keepdims=True)
        col_ref[start : start + HALF, :] = jnp.broadcast_to(
            jnp.sum(energies, axis=1, keepdims=True), (HALF, 128)
        )
    other = pl.multiple_of((1 - mine) * HALF, HALF)
    scale = lax.rsqrt(jnp.maximum(col_ref[pl.ds(other, HALF), 0:1], TINY)) * lax.rsqrt(
        jnp.maximum(msg_ref[0:1, :], TINY)
    )
    for part in range(2):
        given_ref[part] = encode(product_ref[1 - mine, part] * scale)
        kept_ref[part] = product_ref[mine, part]
    again.wait()


def row_energies(load, blocks):
    rows = []
    for block in range(blocks):
        total = jnp.zeros((CR, HALF), jnp.float32)
        for part in range(2):
            for d in range(BAND):
                wide = load(part, d, block).astype(jnp.float32)
                total += wide * wide
        folded = jnp.transpose(total[:, :128] + total[:, 128:])
        rows.append(jnp.sum(folded, axis=0, keepdims=True))
    return jnp.concatenate(rows, axis=1)


def pair_kernel(j, unit, pos_ref, band_ref, own_ref, far_ref, shift_ref, own_m, *rest):
    if (j, unit) == (0, 0):
        kept_ref, given_ref, pair_m, col_ref = rest
        pair_m[...] = jnp.zeros_like(pair_m)
    else:
        before_m, *rest = rest
        if unit == 1:
            near_ref, *rest = rest
        kept_ref, given_ref, pair_m, col_ref = rest
        pair_m[...] = before_m[...]
    core = pos_ref[0]
    mine = pos_ref[1]

    def far_block(part, k, half):
        start = pl.multiple_of(((part * BAND + k) * 2 + half) * CR, CR)
        return far_ref[pl.ds(start, CR), :]

    def far_chunk(part, k):
        start = pl.multiple_of((part * BAND + k) * 2 * CR, 2 * CR)
        return far_ref[pl.ds(start, 2 * CR), :]

    if unit == 0:
        pair_m[1:2, : 2 * CR] = row_energies(far_block, 2)
    elif j == 0:
        pair_m[0:1, :] = row_energies(
            lambda part, d, block: near_ref[part, d, block * CR : block * CR + CR, :], TS // CR
        )
    own_row = own_m[0:1, :]
    near_row = pair_m[0:1, :]
    far_row = pair_m[1:2, : 2 * CR]
    given_ref[TILES * CR :, :] = jnp.zeros((32, HALF), jnp.bfloat16)
    put_energies((own_row, near_row, pair_m[1:2, :]), given_ref)

    def aligned(load, part, s):
        blocks = []
        for d in range(BAND):
            block = load(part, jnp.maximum(d - s, 0))
            if d < 2:
                block = jnp.where(d >= s, block, jnp.zeros_like(block))
            blocks.append(block)
        return jnp.concatenate(blocks, axis=1)

    def chunk_of_rows(ref):
        def load(part, k):
            return jnp.concatenate(
                [ref[part, k, h * HALF + j * CR : h * HALF + j * CR + CR, :] for h in range(2)],
                axis=0,
            )
        return load

    def emit(keep, real, imag, start, rows, row, split):
        for part, value in enumerate((real, imag)):
            if not keep:
                value = encode(value * (col_ref[pl.ds(start, rows), 0:1] * row))
            for tile in range(2):
                if keep:
                    kept_ref[part, tile] = split(value, tile)
                else:
                    given_ref[tile_rows(part, tile), :] = split(value, tile)

    @pl.when(core == 0)
    def _():
        col_ref[...] = column(inverse(own_row))
        if unit == 0:
            load, energy = far_chunk, far_row
        else:
            load, energy = chunk_of_rows(near_ref), chunk_of_lanes(near_row, j)
        s = live_before(band_ref, pos_ref[2] + 2 - unit)
        right_re = aligned(load, 0, s)
        right_im = aligned(load, 1, s)
        row = inverse(energy)
        for keep in (False, True):
            start = pl.multiple_of((mine if keep else 1 - mine) * HALF, HALF)
            left = jnp.concatenate(
                [
                    jnp.concatenate(
                        [own_ref[part, d, pl.ds(start, HALF), :] for d in range(BAND)], axis=1
                    )
                    for part in range(2)
                ],
                axis=0,
            )
            real, imag = complex_product(left, right_re, right_im)
            emit(keep, real, imag, start, HALF, row, lambda v, t: v[t * CR : t * CR + CR])

    @pl.when(core == 1)
    def _():
        col_ref[: 2 * CR, :] = column(inverse(far_row))
        shifts = shift_ref[ROWS:, :].astype(jnp.float32)
        right_ref, energy = (own_ref, own_row) if unit == 0 else (near_ref, near_row)
        s = jnp.max(shifts[2 - unit : 3 - unit, :]).astype(jnp.int32)
        load = lambda part, k: right_ref[part, k]
        right_re = aligned(load, 0, s)
        right_im = aligned(load, 1, s)
        row = inverse(energy)
        for keep in (False, True):
            half = mine if keep else 1 - mine
            left = jnp.concatenate(
                [
                    jnp.concatenate([far_block(part, d, half) for d in range(BAND)], axis=1)
                    for part in range(2)
                ],
                axis=0,
            )
            real, imag = complex_product(left, right_re, right_im)
            start = pl.multiple_of(half * CR, CR)
            emit(keep, real, imag, start, CR, row, lambda v, t: v[:, t * HALF : t * HALF + HALF])


def decode_kernel(j, units, pos_ref, own_m, pair_m, *rest):
    kepts = rest[: len(units)]
    gots = rest[len(units) : 2 * len(units)]
    fin_ref, col_ref = rest[2 * len(units) :]
    core = pos_ref[0]
    mine = pos_ref[1]
    for n, (unit, kept_ref, got_ref) in enumerate(zip(units, kepts, gots)):
        other = [get_energy(got_ref, i) for i in range(3)]
        total = [m + o for m, o in zip((own_m[0:1, :], pair_m[0:1, :], pair_m[1:2, :]), other)]
        root = [jnp.sqrt(jnp.maximum(o, TINY)) for o in other]

        def emit(tile, start, root_row, total_row):
            back = col_ref[0, pl.ds(start, CR), 0:1] * root_row
            scale = lax.rsqrt(col_ref[1, pl.ds(start, CR), 0:1] * total_row + EPSILON)
            for part in range(2):
                value = kept_ref[part, tile] + decode(got_ref[tile_rows(part, tile), :]) * back
                fin_ref[n, part, tile] = (value * scale).astype(jnp.bfloat16)

        @pl.when(core == 0)
        def _():
            col_ref[0] = column(root[0])
            col_ref[1] = column(total[0])
            for tile in range(2):
                start = pl.multiple_of(mine * HALF + tile * CR, CR)
                if unit == 0:
                    emit(tile, start, root[2][:, : 2 * CR], total[2][:, : 2 * CR])
                else:
                    emit(tile, start, chunk_of_lanes(root[1], j), chunk_of_lanes(total[1], j))

        @pl.when(core == 1)
        def _():
            col_ref[0] = column(root[2])
            col_ref[1] = column(total[2])
            start = pl.multiple_of(mine * CR, CR)
            i = 0 if unit == 0 else 1
            for tile in range(2):
                lanes = slice(tile * HALF, tile * HALF + HALF)
                emit(tile, start, root[i][:, lanes], total[i][:, lanes])


def place_copies(core, j, unit, source_ref, out_ref, sem):
    copies = []
    for part in range(2):
        for tile in range(2):
            at = out_ref.at[part, 0, 2 - unit]
            piece = source_ref.at[part, tile]
            n = part * 2 + tile
            if core == 1:
                target = at.at[pl.ds(j * CR, CR), pl.ds(tile * HALF, HALF)]
                copies.append(pltpu.make_async_copy(piece, target, sem.at[n]))
            else:
                for h in range(2):
                    target = at.at[pl.ds(tile * CR, CR), pl.ds(h * HALF + j * CR, CR)]
                    source = piece.at[:, pl.ds(h * CR, CR)]
                    copies.append(pltpu.make_async_copy(source, target, sem.at[2 * n + h]))
    return copies


def finish_kernel(
    pos_ref, kept_ref, got_ref, mine_ref, first_ref, fin0, fin1, back0, back1,
    out_ref, fin_ref, col_ref, sem, place_sem,
):
    places = ((0, 0, 0, 0), (0, 1, 0, 1), (1, 0, 1, 0))
    for wait in (False, True):
        for core, sources in enumerate(((fin0, fin1), (back0, back1))):
            @pl.when(pos_ref[0] == core)
            def _():
                for n, (j, unit, source, slot) in enumerate(places):
                    for copy in place_copies(
                        core, j, unit, sources[source].at[slot], out_ref, place_sem.at[n]
                    ):
                        if wait:
                            copy.wait()
                        else:
                            copy.start()
        if wait:
            break
        start = pl.multiple_of(pos_ref[1] * HALF, HALF)
        energy = get_energy(first_ref, 0)
        other = jnp.sqrt(jnp.maximum(energy, TINY))
        total = mine_ref[0:1, :] + energy
        col_ref[0] = column(other)
        col_ref[1] = column(total)
        scale = lax.rsqrt(col_ref[1, pl.ds(start, HALF), 0:1] * total + EPSILON)
        back = col_ref[0, pl.ds(start, HALF), 0:1] * other
        for part in range(2):
            value = (kept_ref[part] + decode(got_ref[part]) * back) * scale
            fin_ref[part] = value.astype(jnp.bfloat16)
        run(
            [
                pltpu.make_async_copy(fin_ref.at[part], out_ref.at[part, 0, 0], sem.at[part])
                for part in range(2)
            ]
        )


def place_kernel(pos_ref, out_in_ref, fin_ref, back_ref, out_ref, sem):
    del out_in_ref
    for core, source in enumerate((fin_ref, back_ref)):
        @pl.when(pos_ref[0] == core)
        def _():
            run(place_copies(core, 1, 1, source.at[0], out_ref, sem))


def call(name, kernel, outs, specs, scratch=(), flops=0, after=None, out_specs=None, aliases=None, vmem=40):
    shapes = [jax.ShapeDtypeStruct(shape, dtype) for shape, dtype in outs]
    body = kernel if after is None else lambda _, *refs: kernel(*refs)
    run = pl.pallas_call(
        body,
        name=name,
        out_shape=shapes if len(shapes) > 1 else shapes[0],
        in_specs=specs if after is None else [ANY, *specs],
        out_specs=out_specs or ([VMEM] * len(shapes) if len(shapes) > 1 else VMEM),
        scratch_shapes=list(scratch),
        compiler_params=pltpu.CompilerParams(vmem_limit_bytes=vmem * MIB),
        input_output_aliases=aliases or {},
        cost_estimate=pl.CostEstimate(flops=flops, bytes_accessed=2**21, transcendentals=0),
    )
    return run if after is None else lambda *args: run(after, *args)


def shards(correlation, band_tiles):
    bf16, f32 = jnp.bfloat16, jnp.float32
    count = lax.axis_size("rows")
    core = lax.axis_index("rows") % 2
    mine = lax.axis_index("freq") % 2
    pos = jnp.stack([core, mine, lax.axis_index("rows")]).astype(jnp.int32)
    own = correlation.reshape(2, BAND, TS, HALF)
    swap = [(i, i ^ 1) for i in range(lax.axis_size("freq"))]
    pair = [(i, i ^ 1) for i in range(count)]
    far_route = [(i + 2, i) for i in range(0, count - 2, 2)] + [(i - 2, i) for i in range(3, count, 2)]
    back_route = [(i, i - 2) for i in range(3, count, 2)]

    half_shape = (2, HALF, TS)
    token = ((8, 128), f32)
    chunk0, after = call(
        "pack",
        pack_kernel,
        [((ROWS + 16, HALF), bf16), token],
        [SMEM, ANY, ANY],
        [pltpu.VMEM((16, HALF), bf16), pltpu.SMEM((1, BAND), jnp.int32), pltpu.SemaphoreType.DMA((18,))],
        vmem=52,
    )(pos, band_tiles, own)
    far0 = lax.ppermute(chunk0, "rows", far_route)
    kept_self, given_self, message, again = call(
        "self",
        self_kernel,
        [(half_shape, f32), (half_shape, bf16), ((8, TS), f32), (own.shape, bf16)],
        [SMEM, VMEM],
        [
            pltpu.VMEM((2, 2, HALF, TS), f32),
            pltpu.VMEM((TS, 128), f32),
            pltpu.SemaphoreType.DMA(()),
        ],
        after=after,
    )(pos, own)
    got_self = lax.ppermute(given_self, "freq", swap)
    chunk1 = call(
        "second",
        second_kernel,
        [((ROWS, HALF), bf16)],
        [VMEM],
        [pltpu.SemaphoreType.DMA((16,))],
        after=given_self,
    )(own)
    far1 = lax.ppermute(chunk1, "rows", far_route)
    near = lax.ppermute(again, "rows", pair)
    far = (far0, far1)

    unit_shape = (2, 2, CR, HALF)
    after = call("order", order_kernel, [token], [ANY], flops=TCOST)(far0)
    units = {}
    pair_m = None
    for j in range(CHUNKS):
        for unit in range(2):
            extra = [] if pair_m is None else [pair_m] + [near] * unit
            kept, given, pair_m = call(
                f"pair{j}{unit}",
                lambda *refs, j=j, unit=unit: pair_kernel(j, unit, *refs),
                [(unit_shape, f32), ((TILES * CR + 32, HALF), bf16), ((8, TS), f32)],
                [SMEM, SMEM] + [VMEM] * (4 + len(extra)),
                [pltpu.VMEM((TS, 128), f32)],
                flops=PCOST,
                after=after,
            )(pos, band_tiles, own, far[j], far0, message, *extra)
            units[j, unit] = kept, lax.ppermute(given, "freq", swap), pair_m
            after = kept
            if (j, unit) == (0, 0):
                after = call("order1", order_kernel, [token], [ANY], flops=FCOST, after=kept)(got_self)

    def finished(name, j, which, after):
        kepts = [units[j, unit][0] for unit in which]
        gots = [units[j, unit][1] for unit in which]
        fin = call(
            name,
            lambda *refs: decode_kernel(j, which, *refs),
            [((len(which), *unit_shape), bf16)],
            [SMEM] + [VMEM] * (2 + 2 * len(which)),
            [pltpu.VMEM((2, TS, 128), f32)],
            after=after,
        )(pos, message, units[j, which[-1]][2], *kepts, *gots)
        return fin, lax.ppermute(fin, "rows", back_route)

    fin0, back0 = finished("decode0", 0, (0, 1), after)
    fin1, back1 = finished("decode1", 1, (0,), fin0)
    fin2, back2 = finished("decode2", 1, (1,), fin1)
    out_shape = ((2, 1, 3, HALF, TS), bf16)
    out = call(
        "finish",
        finish_kernel,
        [out_shape],
        [SMEM] + [VMEM] * 8,
        [
            pltpu.VMEM((2, HALF, TS), bf16),
            pltpu.VMEM((2, TS, 128), f32),
            pltpu.SemaphoreType.DMA((2,)),
            pltpu.SemaphoreType.DMA((3, 8)),
        ],
        after=fin2,
        out_specs=ANY,
    )(pos, kept_self, got_self, message, units[0, 0][1], fin0, fin1, back0, back1)
    return call(
        "place",
        place_kernel,
        [out_shape],
        [SMEM, ANY, VMEM, VMEM],
        [pltpu.SemaphoreType.DMA((8,))],
        out_specs=ANY,
        aliases={1: 0},
    )(pos, out, fin2, back2)


def solution(mesh):
    return jax.shard_map(
        shards,
        mesh=mesh,
        in_specs=(P(None, "rows", None, None, "freq"), P("rows", None)),
        out_specs=P(None, "rows", None, "freq", None),
        check_vma=False,
    )
```

```python
import jax
import jax.numpy as jnp
from jax import lax
from jax.experimental import pallas as pl
from jax.experimental.pallas import tpu as pltpu
from jax.sharding import PartitionSpec as P

TS = 512
HALF = 256
BAND = 4
CHUNKS = 2
CR = HALF // CHUNKS
TILES = 4
ROWS = 2 * BAND * 2 * CR
EPSILON = 1e-06
TINY = 1e-30
CODE = 2.0**7.5
VMEM = pl.BlockSpec(memory_space=pltpu.VMEM)
ANY = pl.BlockSpec(memory_space=pl.ANY)
SMEM = pl.BlockSpec(memory_space=pltpu.SMEM)
MIB = 1024 * 1024
PCOST = 0
TCOST = 2**32
FCOST = 2**35


def encode(x):
    u = x * CODE
    y = u * u
    y = y * y
    y = y * y
    y = y * y
    return jnp.where(u < 0, -y, y).astype(jnp.bfloat16)


def decode(y):
    y = y.astype(jnp.float32)
    r = lax.rsqrt(lax.rsqrt(lax.rsqrt(lax.rsqrt(jnp.abs(y))))) * (1.0 / CODE)
    return jnp.where(y < 0, -r, r)


def column(row):
    width = row.shape[1]
    return jnp.transpose(jnp.broadcast_to(row, (128, width)))


def tile_rows(part, tile):
    return pl.ds((part * 2 + tile) * CR, CR)


def put_energies(messages, given_ref):
    for i, message in enumerate(messages):
        rest = message
        for level in range(3):
            term = rest.astype(jnp.bfloat16)
            rest = rest - term.astype(jnp.float32)
            for h in range(2):
                row = TILES * CR + (i * 3 + level) * 2 + h
                given_ref[row : row + 1, :] = term[:, h * HALF : h * HALF + HALF]


def get_energy(got_ref, i):
    tail = got_ref[TILES * CR :, :].astype(jnp.float32)
    halves = []
    for h in range(2):
        rows = [tail[(i * 3 + level) * 2 + h :][:1] for level in range(3)]
        halves.append(rows[0] + (rows[1] + rows[2]))
    return jnp.concatenate(halves, axis=1)


def inverse(energy):
    return lax.rsqrt(jnp.maximum(energy, TINY))


def chunk_of_lanes(row, j):
    return jnp.concatenate(
        [row[:, h * HALF + j * CR : h * HALF + j * CR + CR] for h in range(2)], axis=1
    )


def complex_product(left, right_re, right_im):
    dims = (((1,), (1,)), ((), ()))
    with_re = lax.dot_general(left, right_re, dims, preferred_element_type=jnp.float32)
    with_im = lax.dot_general(left, right_im, dims, preferred_element_type=jnp.float32)
    rows = left.shape[0] // 2
    return with_re[:rows] + with_im[rows:], with_re[rows:] - with_im[:rows]


def live_before(band_ref, tile):
    return sum((band_ref[0, d] < tile).astype(jnp.int32) for d in range(BAND))


def run(copies):
    for copy in copies:
        copy.start()
    for copy in copies:
        copy.wait()


def pack_kernel(pos_ref, tiles_ref, own_ref, chunk0_ref, token_ref, shift_ref, band_ref, sem):
    bands = pltpu.make_async_copy(tiles_ref, band_ref, sem.at[17])
    bands.start()
    copies = [
        pltpu.make_async_copy(
            own_ref.at[part, d, pl.ds(half * HALF, CR), :],
            chunk0_ref.at[pl.ds(((part * BAND + d) * 2 + half) * CR, CR), :],
            sem.at[(part * BAND + d) * 2 + half],
        )
        for part in range(2)
        for d in range(BAND)
        for half in range(2)
    ]
    for copy in copies:
        copy.start()
    token_ref[...] = jnp.zeros_like(token_ref)
    shift_ref[...] = jnp.zeros_like(shift_ref)
    bands.wait()
    for offset in (1, 2):
        count = live_before(band_ref, pos_ref[2] + offset).astype(jnp.float32)
        shift_ref[offset : offset + 1, :] = jnp.full((1, HALF), count).astype(jnp.bfloat16)
    run([pltpu.make_async_copy(shift_ref, chunk0_ref.at[pl.ds(ROWS, 16), :], sem.at[16])])
    for copy in copies:
        copy.wait()


def order_kernel(*refs):
    token_ref = refs[-1]
    token_ref[...] = jnp.zeros_like(token_ref)


def self_kernel(
    pos_ref, own_ref, kept_ref, given_ref, msg_ref, again_ref, chunk1_ref, product_ref, col_ref, sem
):
    mine = pos_ref[1]
    copies = [pltpu.make_async_copy(own_ref, again_ref, sem.at[16])]
    copies += [
        pltpu.make_async_copy(
            own_ref.at[part, d, pl.ds(half * HALF + CR, CR), :],
            chunk1_ref.at[pl.ds(((part * BAND + d) * 2 + half) * CR, CR), :],
            sem.at[(part * BAND + d) * 2 + half],
        )
        for part in range(2)
        for d in range(BAND)
        for half in range(2)
    ]
    for copy in copies:
        copy.start()
    msg_ref[...] = jnp.zeros_like(msg_ref)
    right_re = jnp.concatenate([own_ref[0, d] for d in range(BAND)], axis=1)
    right_im = jnp.concatenate([own_ref[1, d] for d in range(BAND)], axis=1)
    diagonal = lax.broadcasted_iota(jnp.int32, (HALF, HALF), 0) == lax.broadcasted_iota(
        jnp.int32, (HALF, HALF), 1
    )
    for half in range(2):
        start = half * HALF
        left = jnp.concatenate(
            [
                jnp.concatenate(
                    [own_ref[part, d, start : start + HALF, :] for d in range(BAND)], axis=1
                )
                for part in range(2)
            ],
            axis=0,
        )
        real, imag = complex_product(left, right_re, right_im)
        product_ref[half, 0] = real
        product_ref[half, 1] = imag
        energies = jnp.where(diagonal, real[:, start : start + HALF], 0.0)
        msg_ref[0:1, start : start + HALF] = jnp.sum(energies, axis=0, keepdims=True)
        col_ref[start : start + HALF, :] = jnp.broadcast_to(
            jnp.sum(energies, axis=1, keepdims=True), (HALF, 128)
        )
    other = pl.multiple_of((1 - mine) * HALF, HALF)
    scale = lax.rsqrt(jnp.maximum(col_ref[pl.ds(other, HALF), 0:1], TINY)) * lax.rsqrt(
        jnp.maximum(msg_ref[0:1, :], TINY)
    )
    for part in range(2):
        given_ref[part] = encode(product_ref[1 - mine, part] * scale)
        kept_ref[part] = product_ref[mine, part]
    for copy in copies:
        copy.wait()


def row_energies(load, blocks):
    rows = []
    for block in range(blocks):
        total = jnp.zeros((CR, HALF), jnp.float32)
        for part in range(2):
            for d in range(BAND):
                wide = load(part, d, block).astype(jnp.float32)
                total += wide * wide
        folded = jnp.transpose(total[:, :128] + total[:, 128:])
        rows.append(jnp.sum(folded, axis=0, keepdims=True))
    return jnp.concatenate(rows, axis=1)


def pair_kernel(j, unit, pos_ref, band_ref, own_ref, far_ref, shift_ref, own_m, *rest):
    if (j, unit) == (0, 0):
        kept_ref, given_ref, pair_m, col_ref = rest
        pair_m[...] = jnp.zeros_like(pair_m)
    else:
        before_m, *rest = rest
        if unit == 1:
            near_ref, *rest = rest
        kept_ref, given_ref, pair_m, col_ref = rest
        pair_m[...] = before_m[...]
    core = pos_ref[0]
    mine = pos_ref[1]

    def far_block(part, k, half):
        start = pl.multiple_of(((part * BAND + k) * 2 + half) * CR, CR)
        return far_ref[pl.ds(start, CR), :]

    def far_chunk(part, k):
        start = pl.multiple_of((part * BAND + k) * 2 * CR, 2 * CR)
        return far_ref[pl.ds(start, 2 * CR), :]

    if unit == 0:
        pair_m[1:2, : 2 * CR] = row_energies(far_block, 2)
    elif j == 0:
        pair_m[0:1, :] = row_energies(
            lambda part, d, block: near_ref[part, d, block * CR : block * CR + CR, :], TS // CR
        )
    own_row = own_m[0:1, :]
    near_row = pair_m[0:1, :]
    far_row = pair_m[1:2, : 2 * CR]
    given_ref[TILES * CR :, :] = jnp.zeros((32, HALF), jnp.bfloat16)
    put_energies((own_row, near_row, pair_m[1:2, :]), given_ref)

    def aligned(load, part, s):
        blocks = []
        for d in range(BAND):
            block = load(part, jnp.maximum(d - s, 0))
            if d < 2:
                block = jnp.where(d >= s, block, jnp.zeros_like(block))
            blocks.append(block)
        return jnp.concatenate(blocks, axis=1)

    def chunk_of_rows(ref):
        def load(part, k):
            return jnp.concatenate(
                [ref[part, k, h * HALF + j * CR : h * HALF + j * CR + CR, :] for h in range(2)],
                axis=0,
            )
        return load

    def emit(keep, real, imag, start, rows, row, split):
        for part, value in enumerate((real, imag)):
            if not keep:
                value = encode(value * (col_ref[pl.ds(start, rows), 0:1] * row))
            for tile in range(2):
                if keep:
                    kept_ref[part, tile] = split(value, tile)
                else:
                    given_ref[tile_rows(part, tile), :] = split(value, tile)

    @pl.when(core == 0)
    def _():
        col_ref[...] = column(inverse(own_row))
        if unit == 0:
            load, energy = far_chunk, far_row
        else:
            load, energy = chunk_of_rows(near_ref), chunk_of_lanes(near_row, j)
        s = live_before(band_ref, pos_ref[2] + 2 - unit)
        right_re = aligned(load, 0, s)
        right_im = aligned(load, 1, s)
        row = inverse(energy)
        for keep in (False, True):
            start = pl.multiple_of((mine if keep else 1 - mine) * HALF, HALF)
            left = jnp.concatenate(
                [
                    jnp.concatenate(
                        [own_ref[part, d, pl.ds(start, HALF), :] for d in range(BAND)], axis=1
                    )
                    for part in range(2)
                ],
                axis=0,
            )
            real, imag = complex_product(left, right_re, right_im)
            emit(keep, real, imag, start, HALF, row, lambda v, t: v[t * CR : t * CR + CR])

    @pl.when(core == 1)
    def _():
        col_ref[: 2 * CR, :] = column(inverse(far_row))
        shifts = shift_ref[ROWS:, :].astype(jnp.float32)
        right_ref, energy = (own_ref, own_row) if unit == 0 else (near_ref, near_row)
        s = jnp.max(shifts[2 - unit : 3 - unit, :]).astype(jnp.int32)
        load = lambda part, k: right_ref[part, k]
        right_re = aligned(load, 0, s)
        right_im = aligned(load, 1, s)
        row = inverse(energy)
        for keep in (False, True):
            half = mine if keep else 1 - mine
            left = jnp.concatenate(
                [
                    jnp.concatenate([far_block(part, d, half) for d in range(BAND)], axis=1)
                    for part in range(2)
                ],
                axis=0,
            )
            real, imag = complex_product(left, right_re, right_im)
            start = pl.multiple_of(half * CR, CR)
            emit(keep, real, imag, start, CR, row, lambda v, t: v[:, t * HALF : t * HALF + HALF])


def decode_kernel(j, units, pos_ref, own_m, pair_m, *rest, first=0):
    kepts = rest[: len(units)]
    gots = rest[len(units) : 2 * len(units)]
    fin_ref, col_ref = rest[2 * len(units) :]
    core = pos_ref[0]
    mine = pos_ref[1]
    for n, (unit, kept_ref, got_ref) in enumerate(zip(units, kepts, gots)):
        other = [get_energy(got_ref, i) for i in range(3)]
        total = [m + o for m, o in zip((own_m[0:1, :], pair_m[0:1, :], pair_m[1:2, :]), other)]
        root = [jnp.sqrt(jnp.maximum(o, TINY)) for o in other]

        def emit(tile, start, root_row, total_row):
            back = col_ref[0, pl.ds(start, CR), 0:1] * root_row
            scale = lax.rsqrt(col_ref[1, pl.ds(start, CR), 0:1] * total_row + EPSILON)
            for part in range(2):
                value = kept_ref[part, tile] + decode(got_ref[tile_rows(part, tile), :]) * back
                fin_ref[first + n, part, tile] = (value * scale).astype(jnp.bfloat16)

        @pl.when(core == 0)
        def _():
            col_ref[0] = column(root[0])
            col_ref[1] = column(total[0])
            for tile in range(2):
                start = pl.multiple_of(mine * HALF + tile * CR, CR)
                if unit == 0:
                    emit(tile, start, root[2][:, : 2 * CR], total[2][:, : 2 * CR])
                else:
                    emit(tile, start, chunk_of_lanes(root[1], j), chunk_of_lanes(total[1], j))

        @pl.when(core == 1)
        def _():
            col_ref[0] = column(root[2])
            col_ref[1] = column(total[2])
            start = pl.multiple_of(mine * CR, CR)
            i = 0 if unit == 0 else 1
            for tile in range(2):
                lanes = slice(tile * HALF, tile * HALF + HALF)
                emit(tile, start, root[i][:, lanes], total[i][:, lanes])


def last_decode_kernel(pos_ref, own_m, pair_m, kept_ref, got_ref, done_ref, fin_ref, col_ref, sem):
    copy = pltpu.make_async_copy(done_ref.at[0], fin_ref.at[0], sem)
    copy.start()
    decode_kernel(1, (1,), pos_ref, own_m, pair_m, kept_ref, got_ref, fin_ref, col_ref, first=1)
    copy.wait()


def place_copies(core, j, unit, source_ref, out_ref, sem):
    copies = []
    for part in range(2):
        for tile in range(2):
            at = out_ref.at[part, 0, 2 - unit]
            piece = source_ref.at[part, tile]
            n = part * 2 + tile
            if core == 1:
                target = at.at[pl.ds(j * CR, CR), pl.ds(tile * HALF, HALF)]
                copies.append(pltpu.make_async_copy(piece, target, sem.at[n]))
            else:
                for h in range(2):
                    target = at.at[pl.ds(tile * CR, CR), pl.ds(h * HALF + j * CR, CR)]
                    source = piece.at[:, pl.ds(h * CR, CR)]
                    copies.append(pltpu.make_async_copy(source, target, sem.at[2 * n + h]))
    return copies


def finish_kernel(
    pos_ref, kept_ref, got_ref, mine_ref, first_ref, fin0, back0, out_ref, fin_ref, col_ref, sem, place_sem
):
    for wait in (False, True):
        for core, source in enumerate((fin0, back0)):
            @pl.when(pos_ref[0] == core)
            def _():
                for unit in range(2):
                    for copy in place_copies(
                        core, 0, unit, source.at[unit], out_ref, place_sem.at[unit]
                    ):
                        if wait:
                            copy.wait()
                        else:
                            copy.start()
        if wait:
            break
        start = pl.multiple_of(pos_ref[1] * HALF, HALF)
        energy = get_energy(first_ref, 0)
        other = jnp.sqrt(jnp.maximum(energy, TINY))
        total = mine_ref[0:1, :] + energy
        col_ref[0] = column(other)
        col_ref[1] = column(total)
        scale = lax.rsqrt(col_ref[1, pl.ds(start, HALF), 0:1] * total + EPSILON)
        back = col_ref[0, pl.ds(start, HALF), 0:1] * other
        for part in range(2):
            value = (kept_ref[part] + decode(got_ref[part]) * back) * scale
            fin_ref[part] = value.astype(jnp.bfloat16)
        run(
            [
                pltpu.make_async_copy(fin_ref.at[part], out_ref.at[part, 0, 0], sem.at[part])
                for part in range(2)
            ]
        )


def place_kernel(pos_ref, out_in_ref, fin_ref, back_ref, out_ref, sem):
    del out_in_ref
    for core, source in enumerate((fin_ref, back_ref)):
        @pl.when(pos_ref[0] == core)
        def _():
            run(
                [
                    copy
                    for unit in range(2)
                    for copy in place_copies(core, 1, unit, source.at[unit], out_ref, sem.at[unit])
                ]
            )


def call(name, kernel, outs, specs, scratch=(), flops=0, after=None, out_specs=None, aliases=None, vmem=40):
    shapes = [jax.ShapeDtypeStruct(shape, dtype) for shape, dtype in outs]
    body = kernel if after is None else lambda _, *refs: kernel(*refs)
    run = pl.pallas_call(
        body,
        name=name,
        out_shape=shapes if len(shapes) > 1 else shapes[0],
        in_specs=specs if after is None else [ANY, *specs],
        out_specs=out_specs or ([VMEM] * len(shapes) if len(shapes) > 1 else VMEM),
        scratch_shapes=list(scratch),
        compiler_params=pltpu.CompilerParams(vmem_limit_bytes=vmem * MIB),
        input_output_aliases=aliases or {},
        cost_estimate=pl.CostEstimate(flops=flops, bytes_accessed=2**21, transcendentals=0),
    )
    return run if after is None else lambda *args: run(after, *args)


def shards(correlation, band_tiles):
    bf16, f32 = jnp.bfloat16, jnp.float32
    count = lax.axis_size("rows")
    core = lax.axis_index("rows") % 2
    mine = lax.axis_index("freq") % 2
    pos = jnp.stack([core, mine, lax.axis_index("rows")]).astype(jnp.int32)
    own = correlation.reshape(2, BAND, TS, HALF)
    swap = [(i, i ^ 1) for i in range(lax.axis_size("freq"))]
    pair = [(i, i ^ 1) for i in range(count)]
    far_route = [(i + 2, i) for i in range(0, count - 2, 2)] + [(i - 2, i) for i in range(3, count, 2)]
    back_route = [(i, i - 2) for i in range(3, count, 2)]

    half_shape = (2, HALF, TS)
    token = ((8, 128), f32)
    chunk0, after = call(
        "pack",
        pack_kernel,
        [((ROWS + 16, HALF), bf16), token],
        [SMEM, ANY, ANY],
        [pltpu.VMEM((16, HALF), bf16), pltpu.SMEM((1, BAND), jnp.int32), pltpu.SemaphoreType.DMA((18,))],
        vmem=52,
    )(pos, band_tiles, own)
    far0 = lax.ppermute(chunk0, "rows", far_route)
    kept_self, given_self, message, again, chunk1 = call(
        "self",
        self_kernel,
        [(half_shape, f32), (half_shape, bf16), ((8, TS), f32), (own.shape, bf16), ((ROWS, HALF), bf16)],
        [SMEM, VMEM],
        [
            pltpu.VMEM((2, 2, HALF, TS), f32),
            pltpu.VMEM((TS, 128), f32),
            pltpu.SemaphoreType.DMA((17,)),
        ],
        after=after,
    )(pos, own)
    got_self = lax.ppermute(given_self, "freq", swap)
    far1 = lax.ppermute(chunk1, "rows", far_route)
    near = lax.ppermute(again, "rows", pair)
    far = (far0, far1)

    unit_shape = (2, 2, CR, HALF)
    after = call("order", order_kernel, [token], [ANY], flops=TCOST)(far0)
    units = {}
    pair_m = None
    for j in range(CHUNKS):
        for unit in range(2):
            extra = [] if pair_m is None else [pair_m] + [near] * unit
            kept, given, pair_m = call(
                f"pair{j}{unit}",
                lambda *refs, j=j, unit=unit: pair_kernel(j, unit, *refs),
                [(unit_shape, f32), ((TILES * CR + 32, HALF), bf16), ((8, TS), f32)],
                [SMEM, SMEM] + [VMEM] * (4 + len(extra)),
                [pltpu.VMEM((TS, 128), f32)],
                flops=PCOST,
                after=after,
            )(pos, band_tiles, own, far[j], far0, message, *extra)
            units[j, unit] = kept, lax.ppermute(given, "freq", swap), pair_m
            after = kept
            if (j, unit) == (0, 0):
                after = call("order1", order_kernel, [token], [ANY], flops=FCOST, after=kept)(got_self)

    def decoded(name, j, which, after):
        return call(
            name,
            lambda *refs: decode_kernel(j, which, *refs),
            [((len(which), *unit_shape), bf16)],
            [SMEM] + [VMEM] * (2 + 2 * len(which)),
            [pltpu.VMEM((2, TS, 128), f32)],
            after=after,
        )(
            pos,
            message,
            units[j, which[-1]][2],
            *[units[j, unit][0] for unit in which],
            *[units[j, unit][1] for unit in which],
        )

    fin0 = decoded("decode0", 0, (0, 1), after)
    back0 = lax.ppermute(fin0, "rows", back_route)
    fin1 = decoded("decode1", 1, (0,), fin0)
    fin2 = call(
        "decode2",
        last_decode_kernel,
        [((2, *unit_shape), bf16)],
        [SMEM] + [VMEM] * 5,
        [pltpu.VMEM((2, TS, 128), f32), pltpu.SemaphoreType.DMA(())],
    )(pos, message, units[1, 1][2], *units[1, 1][:2], fin1)
    back2 = lax.ppermute(fin2, "rows", back_route)
    out_shape = ((2, 1, 3, HALF, TS), bf16)
    out = call(
        "finish",
        finish_kernel,
        [out_shape],
        [SMEM] + [VMEM] * 6,
        [
            pltpu.VMEM((2, HALF, TS), bf16),
            pltpu.VMEM((2, TS, 128), f32),
            pltpu.SemaphoreType.DMA((2,)),
            pltpu.SemaphoreType.DMA((2, 8)),
        ],
        after=fin2,
        out_specs=ANY,
    )(pos, kept_self, got_self, message, units[0, 0][1], fin0, back0)
    return call(
        "place",
        place_kernel,
        [out_shape],
        [SMEM, ANY, VMEM, VMEM],
        [pltpu.SemaphoreType.DMA((2, 8))],
        out_specs=ANY,
        aliases={1: 0},
    )(pos, out, fin2, back2)


def solution(mesh):
    return jax.shard_map(
        shards,
        mesh=mesh,
        in_specs=(P(None, "rows", None, None, "freq"), P("rows", None)),
        out_specs=P(None, "rows", None, "freq", None),
        check_vma=False,
    )
```

```python
import jax
import jax.numpy as jnp
from jax import lax
from jax.experimental import pallas as pl
from jax.experimental.pallas import tpu as pltpu
from jax.sharding import PartitionSpec as P

TS = 512
HALF = 256
BAND = 4
CHUNKS = 2
CR = HALF // CHUNKS
TILES = 4
ROWS = 2 * BAND * 2 * CR
EPSILON = 1e-06
TINY = 1e-30
CODE = 2.0**7.5
VMEM = pl.BlockSpec(memory_space=pltpu.VMEM)
ANY = pl.BlockSpec(memory_space=pl.ANY)
SMEM = pl.BlockSpec(memory_space=pltpu.SMEM)
MIB = 1024 * 1024
PCOST = 0
TCOST = 2**32
FCOST = 2**35


def encode(x):
    u = x * CODE
    y = u * u
    y = y * y
    y = y * y
    y = y * y
    return jnp.where(u < 0, -y, y).astype(jnp.bfloat16)


def decode(y):
    y = y.astype(jnp.float32)
    r = lax.rsqrt(lax.rsqrt(lax.rsqrt(lax.rsqrt(jnp.abs(y))))) * (1.0 / CODE)
    return jnp.where(y < 0, -r, r)


def column(row):
    width = row.shape[1]
    return jnp.transpose(jnp.broadcast_to(row, (128, width)))


def tile_rows(part, tile):
    return pl.ds((part * 2 + tile) * CR, CR)


def put_energies(messages, given_ref):
    for i, message in enumerate(messages):
        rest = message
        for level in range(3):
            term = rest.astype(jnp.bfloat16)
            rest = rest - term.astype(jnp.float32)
            for h in range(2):
                row = TILES * CR + (i * 3 + level) * 2 + h
                given_ref[row : row + 1, :] = term[:, h * HALF : h * HALF + HALF]


def get_energy(got_ref, i):
    tail = got_ref[TILES * CR :, :].astype(jnp.float32)
    halves = []
    for h in range(2):
        rows = [tail[(i * 3 + level) * 2 + h :][:1] for level in range(3)]
        halves.append(rows[0] + (rows[1] + rows[2]))
    return jnp.concatenate(halves, axis=1)


def inverse(energy):
    return lax.rsqrt(jnp.maximum(energy, TINY))


def chunk_of_lanes(row, j):
    return jnp.concatenate(
        [row[:, h * HALF + j * CR : h * HALF + j * CR + CR] for h in range(2)], axis=1
    )


def complex_product(left, right_re, right_im):
    rows = left.shape[0] // 2
    real, imag = left[:rows], left[rows:]
    both = jnp.concatenate(
        [jnp.concatenate([real, imag], axis=1), jnp.concatenate([imag, -real], axis=1)], axis=0
    )
    right = jnp.concatenate([right_re, right_im], axis=1)
    product = lax.dot_general(
        both, right, (((1,), (1,)), ((), ())), preferred_element_type=jnp.float32
    )
    return product[:rows], product[rows:]


def live_before(band_ref, tile):
    return sum((band_ref[0, d] < tile).astype(jnp.int32) for d in range(BAND))


def run(copies):
    for copy in copies:
        copy.start()
    for copy in copies:
        copy.wait()


def pack_kernel(pos_ref, tiles_ref, own_ref, chunk0_ref, token_ref, shift_ref, band_ref, sem):
    bands = pltpu.make_async_copy(tiles_ref, band_ref, sem.at[17])
    bands.start()
    copies = [
        pltpu.make_async_copy(
            own_ref.at[part, d, pl.ds(half * HALF, CR), :],
            chunk0_ref.at[pl.ds(((part * BAND + d) * 2 + half) * CR, CR), :],
            sem.at[(part * BAND + d) * 2 + half],
        )
        for part in range(2)
        for d in range(BAND)
        for half in range(2)
    ]
    for copy in copies:
        copy.start()
    token_ref[...] = jnp.zeros_like(token_ref)
    shift_ref[...] = jnp.zeros_like(shift_ref)
    bands.wait()
    for offset in (1, 2):
        count = live_before(band_ref, pos_ref[2] + offset).astype(jnp.float32)
        shift_ref[offset : offset + 1, :] = jnp.full((1, HALF), count).astype(jnp.bfloat16)
    run([pltpu.make_async_copy(shift_ref, chunk0_ref.at[pl.ds(ROWS, 16), :], sem.at[16])])
    for copy in copies:
        copy.wait()


def order_kernel(*refs):
    token_ref = refs[-1]
    token_ref[...] = jnp.zeros_like(token_ref)


def second_kernel(own_ref, chunk1_ref):
    for part in range(2):
        for d in range(BAND):
            for half in range(2):
                row = ((part * BAND + d) * 2 + half) * CR
                start = half * HALF + CR
                chunk1_ref[row : row + CR, :] = own_ref[part, d, start : start + CR, :]


def self_kernel(
    pos_ref, own_ref, kept_ref, given_ref, msg_ref, again_ref, product_ref, col_ref, sem
):
    mine = pos_ref[1]
    again = pltpu.make_async_copy(own_ref, again_ref, sem)
    again.start()
    msg_ref[...] = jnp.zeros_like(msg_ref)
    right_re = jnp.concatenate([own_ref[0, d] for d in range(BAND)], axis=1)
    right_im = jnp.concatenate([own_ref[1, d] for d in range(BAND)], axis=1)
    diagonal = lax.broadcasted_iota(jnp.int32, (HALF, HALF), 0) == lax.broadcasted_iota(
        jnp.int32, (HALF, HALF), 1
    )
    for half in range(2):
        start = half * HALF
        left = jnp.concatenate(
            [
                jnp.concatenate(
                    [own_ref[part, d, start : start + HALF, :] for d in range(BAND)], axis=1
                )
                for part in range(2)
            ],
            axis=0,
        )
        real, imag = complex_product(left, right_re, right_im)
        product_ref[half, 0] = real
        product_ref[half, 1] = imag
        energies = jnp.where(diagonal, real[:, start : start + HALF], 0.0)
        msg_ref[0:1, start : start + HALF] = jnp.sum(energies, axis=0, keepdims=True)
        col_ref[start : start + HALF, :] = jnp.broadcast_to(
            jnp.sum(energies, axis=1, keepdims=True), (HALF, 128)
        )
    other = pl.multiple_of((1 - mine) * HALF, HALF)
    scale = lax.rsqrt(jnp.maximum(col_ref[pl.ds(other, HALF), 0:1], TINY)) * lax.rsqrt(
        jnp.maximum(msg_ref[0:1, :], TINY)
    )
    for part in range(2):
        given_ref[part] = encode(product_ref[1 - mine, part] * scale)
        kept_ref[part] = product_ref[mine, part]
    again.wait()


def row_energies(load, blocks):
    rows = []
    for block in range(blocks):
        total = jnp.zeros((CR, HALF), jnp.float32)
        for part in range(2):
            for d in range(BAND):
                wide = load(part, d, block).astype(jnp.float32)
                total += wide * wide
        folded = jnp.transpose(total[:, :128] + total[:, 128:])
        rows.append(jnp.sum(folded, axis=0, keepdims=True))
    return jnp.concatenate(rows, axis=1)


def pair_kernel(j, unit, pos_ref, band_ref, own_ref, far_ref, shift_ref, own_m, *rest):
    if (j, unit) == (0, 0):
        kept_ref, given_ref, pair_m, col_ref = rest
        pair_m[...] = jnp.zeros_like(pair_m)
    else:
        before_m, *rest = rest
        if unit == 1:
            near_ref, *rest = rest
        kept_ref, given_ref, pair_m, col_ref = rest
        pair_m[...] = before_m[...]
    core = pos_ref[0]
    mine = pos_ref[1]

    def far_block(part, k, half):
        start = pl.multiple_of(((part * BAND + k) * 2 + half) * CR, CR)
        return far_ref[pl.ds(start, CR), :]

    def far_chunk(part, k):
        start = pl.multiple_of((part * BAND + k) * 2 * CR, 2 * CR)
        return far_ref[pl.ds(start, 2 * CR), :]

    if unit == 0:
        pair_m[1:2, : 2 * CR] = row_energies(far_block, 2)
    elif j == 0:
        pair_m[0:1, :] = row_energies(
            lambda part, d, block: near_ref[part, d, block * CR : block * CR + CR, :], TS // CR
        )
    own_row = own_m[0:1, :]
    near_row = pair_m[0:1, :]
    far_row = pair_m[1:2, : 2 * CR]
    given_ref[TILES * CR :, :] = jnp.zeros((32, HALF), jnp.bfloat16)
    put_energies((own_row, near_row, pair_m[1:2, :]), given_ref)

    def aligned(load, part, s):
        blocks = []
        for d in range(BAND):
            block = load(part, jnp.maximum(d - s, 0))
            if d < 2:
                block = jnp.where(d >= s, block, jnp.zeros_like(block))
            blocks.append(block)
        return jnp.concatenate(blocks, axis=1)

    def chunk_of_rows(ref):
        def load(part, k):
            return jnp.concatenate(
                [ref[part, k, h * HALF + j * CR : h * HALF + j * CR + CR, :] for h in range(2)],
                axis=0,
            )
        return load

    def emit(keep, real, imag, start, rows, row, split):
        for part, value in enumerate((real, imag)):
            if not keep:
                value = encode(value * (col_ref[pl.ds(start, rows), 0:1] * row))
            for tile in range(2):
                if keep:
                    kept_ref[part, tile] = split(value, tile)
                else:
                    given_ref[tile_rows(part, tile), :] = split(value, tile)

    @pl.when(core == 0)
    def _():
        col_ref[...] = column(inverse(own_row))
        if unit == 0:
            load, energy = far_chunk, far_row
        else:
            load, energy = chunk_of_rows(near_ref), chunk_of_lanes(near_row, j)
        s = live_before(band_ref, pos_ref[2] + 2 - unit)
        right_re = aligned(load, 0, s)
        right_im = aligned(load, 1, s)
        row = inverse(energy)
        for keep in (False, True):
            start = pl.multiple_of((mine if keep else 1 - mine) * HALF, HALF)
            left = jnp.concatenate(
                [
                    jnp.concatenate(
                        [own_ref[part, d, pl.ds(start, HALF), :] for d in range(BAND)], axis=1
                    )
                    for part in range(2)
                ],
                axis=0,
            )
            real, imag = complex_product(left, right_re, right_im)
            emit(keep, real, imag, start, HALF, row, lambda v, t: v[t * CR : t * CR + CR])

    @pl.when(core == 1)
    def _():
        col_ref[: 2 * CR, :] = column(inverse(far_row))
        shifts = shift_ref[ROWS:, :].astype(jnp.float32)
        right_ref, energy = (own_ref, own_row) if unit == 0 else (near_ref, near_row)
        s = jnp.max(shifts[2 - unit : 3 - unit, :]).astype(jnp.int32)
        load = lambda part, k: right_ref[part, k]
        right_re = aligned(load, 0, s)
        right_im = aligned(load, 1, s)
        row = inverse(energy)
        for keep in (False, True):
            half = mine if keep else 1 - mine
            left = jnp.concatenate(
                [
                    jnp.concatenate([far_block(part, d, half) for d in range(BAND)], axis=1)
                    for part in range(2)
                ],
                axis=0,
            )
            real, imag = complex_product(left, right_re, right_im)
            start = pl.multiple_of(half * CR, CR)
            emit(keep, real, imag, start, CR, row, lambda v, t: v[:, t * HALF : t * HALF + HALF])


def decode_kernel(j, units, pos_ref, own_m, pair_m, *rest):
    kepts = rest[: len(units)]
    gots = rest[len(units) : 2 * len(units)]
    fin_ref, col_ref = rest[2 * len(units) :]
    core = pos_ref[0]
    mine = pos_ref[1]
    for n, (unit, kept_ref, got_ref) in enumerate(zip(units, kepts, gots)):
        other = [get_energy(got_ref, i) for i in range(3)]
        total = [m + o for m, o in zip((own_m[0:1, :], pair_m[0:1, :], pair_m[1:2, :]), other)]
        root = [jnp.sqrt(jnp.maximum(o, TINY)) for o in other]

        def emit(tile, start, root_row, total_row):
            back = col_ref[0, pl.ds(start, CR), 0:1] * root_row
            scale = lax.rsqrt(col_ref[1, pl.ds(start, CR), 0:1] * total_row + EPSILON)
            for part in range(2):
                value = kept_ref[part, tile] + decode(got_ref[tile_rows(part, tile), :]) * back
                fin_ref[n, part, tile] = (value * scale).astype(jnp.bfloat16)

        @pl.when(core == 0)
        def _():
            col_ref[0] = column(root[0])
            col_ref[1] = column(total[0])
            for tile in range(2):
                start = pl.multiple_of(mine * HALF + tile * CR, CR)
                if unit == 0:
                    emit(tile, start, root[2][:, : 2 * CR], total[2][:, : 2 * CR])
                else:
                    emit(tile, start, chunk_of_lanes(root[1], j), chunk_of_lanes(total[1], j))

        @pl.when(core == 1)
        def _():
            col_ref[0] = column(root[2])
            col_ref[1] = column(total[2])
            start = pl.multiple_of(mine * CR, CR)
            i = 0 if unit == 0 else 1
            for tile in range(2):
                lanes = slice(tile * HALF, tile * HALF + HALF)
                emit(tile, start, root[i][:, lanes], total[i][:, lanes])


def place_copies(core, j, unit, source_ref, out_ref, sem):
    copies = []
    for part in range(2):
        for tile in range(2):
            at = out_ref.at[part, 0, 2 - unit]
            piece = source_ref.at[part, tile]
            n = part * 2 + tile
            if core == 1:
                target = at.at[pl.ds(j * CR, CR), pl.ds(tile * HALF, HALF)]
                copies.append(pltpu.make_async_copy(piece, target, sem.at[n]))
            else:
                for h in range(2):
                    target = at.at[pl.ds(tile * CR, CR), pl.ds(h * HALF + j * CR, CR)]
                    source = piece.at[:, pl.ds(h * CR, CR)]
                    copies.append(pltpu.make_async_copy(source, target, sem.at[2 * n + h]))
    return copies


def finish_kernel(
    pos_ref, kept_ref, got_ref, mine_ref, first_ref, fin0, fin1, back0, back1,
    out_ref, fin_ref, col_ref, sem, place_sem,
):
    places = ((0, 0, 0, 0), (0, 1, 0, 1), (1, 0, 1, 0))
    for wait in (False, True):
        for core, sources in enumerate(((fin0, fin1), (back0, back1))):
            @pl.when(pos_ref[0] == core)
            def _():
                for n, (j, unit, source, slot) in enumerate(places):
                    for copy in place_copies(
                        core, j, unit, sources[source].at[slot], out_ref, place_sem.at[n]
                    ):
                        if wait:
                            copy.wait()
                        else:
                            copy.start()
        if wait:
            break
        start = pl.multiple_of(pos_ref[1] * HALF, HALF)
        energy = get_energy(first_ref, 0)
        other = jnp.sqrt(jnp.maximum(energy, TINY))
        total = mine_ref[0:1, :] + energy
        col_ref[0] = column(other)
        col_ref[1] = column(total)
        scale = lax.rsqrt(col_ref[1, pl.ds(start, HALF), 0:1] * total + EPSILON)
        back = col_ref[0, pl.ds(start, HALF), 0:1] * other
        for part in range(2):
            value = (kept_ref[part] + decode(got_ref[part]) * back) * scale
            fin_ref[part] = value.astype(jnp.bfloat16)
        run(
            [
                pltpu.make_async_copy(fin_ref.at[part], out_ref.at[part, 0, 0], sem.at[part])
                for part in range(2)
            ]
        )


def place_kernel(pos_ref, out_in_ref, fin_ref, back_ref, out_ref, sem):
    del out_in_ref
    for core, source in enumerate((fin_ref, back_ref)):
        @pl.when(pos_ref[0] == core)
        def _():
            run(place_copies(core, 1, 1, source.at[0], out_ref, sem))


def call(name, kernel, outs, specs, scratch=(), flops=0, after=None, out_specs=None, aliases=None, vmem=40):
    shapes = [jax.ShapeDtypeStruct(shape, dtype) for shape, dtype in outs]
    body = kernel if after is None else lambda _, *refs: kernel(*refs)
    run = pl.pallas_call(
        body,
        name=name,
        out_shape=shapes if len(shapes) > 1 else shapes[0],
        in_specs=specs if after is None else [ANY, *specs],
        out_specs=out_specs or ([VMEM] * len(shapes) if len(shapes) > 1 else VMEM),
        scratch_shapes=list(scratch),
        compiler_params=pltpu.CompilerParams(vmem_limit_bytes=vmem * MIB),
        input_output_aliases=aliases or {},
        cost_estimate=pl.CostEstimate(flops=flops, bytes_accessed=2**21, transcendentals=0),
    )
    return run if after is None else lambda *args: run(after, *args)


def shards(correlation, band_tiles):
    bf16, f32 = jnp.bfloat16, jnp.float32
    count = lax.axis_size("rows")
    core = lax.axis_index("rows") % 2
    mine = lax.axis_index("freq") % 2
    pos = jnp.stack([core, mine, lax.axis_index("rows")]).astype(jnp.int32)
    own = correlation.reshape(2, BAND, TS, HALF)
    swap = [(i, i ^ 1) for i in range(lax.axis_size("freq"))]
    pair = [(i, i ^ 1) for i in range(count)]
    far_route = [(i + 2, i) for i in range(0, count - 2, 2)] + [(i - 2, i) for i in range(3, count, 2)]
    back_route = [(i, i - 2) for i in range(3, count, 2)]

    half_shape = (2, HALF, TS)
    token = ((8, 128), f32)
    chunk0, after = call(
        "pack",
        pack_kernel,
        [((ROWS + 16, HALF), bf16), token],
        [SMEM, ANY, ANY],
        [pltpu.VMEM((16, HALF), bf16), pltpu.SMEM((1, BAND), jnp.int32), pltpu.SemaphoreType.DMA((18,))],
        vmem=52,
    )(pos, band_tiles, own)
    far0 = lax.ppermute(chunk0, "rows", far_route)
    kept_self, given_self, message, again = call(
        "self",
        self_kernel,
        [(half_shape, f32), (half_shape, bf16), ((8, TS), f32), (own.shape, bf16)],
        [SMEM, VMEM],
        [
            pltpu.VMEM((2, 2, HALF, TS), f32),
            pltpu.VMEM((TS, 128), f32),
            pltpu.SemaphoreType.DMA(()),
        ],
        after=after,
    )(pos, own)
    got_self = lax.ppermute(given_self, "freq", swap)
    chunk1 = call(
        "second",
        second_kernel,
        [((ROWS, HALF), bf16)],
        [VMEM],
        after=given_self,
    )(own)
    far1 = lax.ppermute(chunk1, "rows", far_route)
    near = lax.ppermute(again, "rows", pair)
    far = (far0, far1)

    unit_shape = (2, 2, CR, HALF)
    after = call("order", order_kernel, [token], [ANY], flops=TCOST)(far0)
    units = {}
    pair_m = None
    for j in range(CHUNKS):
        for unit in range(2):
            extra = [] if pair_m is None else [pair_m] + [near] * unit
            kept, given, pair_m = call(
                f"pair{j}{unit}",
                lambda *refs, j=j, unit=unit: pair_kernel(j, unit, *refs),
                [(unit_shape, f32), ((TILES * CR + 32, HALF), bf16), ((8, TS), f32)],
                [SMEM, SMEM] + [VMEM] * (4 + len(extra)),
                [pltpu.VMEM((TS, 128), f32)],
                flops=PCOST,
                after=after,
            )(pos, band_tiles, own, far[j], far0, message, *extra)
            units[j, unit] = kept, lax.ppermute(given, "freq", swap), pair_m
            after = kept
            if (j, unit) == (0, 0):
                after = call("order1", order_kernel, [token], [ANY], flops=FCOST, after=kept)(got_self)

    def finished(name, j, which, after):
        kepts = [units[j, unit][0] for unit in which]
        gots = [units[j, unit][1] for unit in which]
        fin = call(
            name,
            lambda *refs: decode_kernel(j, which, *refs),
            [((len(which), *unit_shape), bf16)],
            [SMEM] + [VMEM] * (2 + 2 * len(which)),
            [pltpu.VMEM((2, TS, 128), f32)],
            after=after,
        )(pos, message, units[j, which[-1]][2], *kepts, *gots)
        return fin, lax.ppermute(fin, "rows", back_route)

    fin0, back0 = finished("decode0", 0, (0, 1), after)
    fin1, back1 = finished("decode1", 1, (0,), fin0)
    fin2, back2 = finished("decode2", 1, (1,), fin1)
    out_shape = ((2, 1, 3, HALF, TS), bf16)
    out = call(
        "finish",
        finish_kernel,
        [out_shape],
        [SMEM] + [VMEM] * 8,
        [
            pltpu.VMEM((2, HALF, TS), bf16),
            pltpu.VMEM((2, TS, 128), f32),
            pltpu.SemaphoreType.DMA((2,)),
            pltpu.SemaphoreType.DMA((3, 8)),
        ],
        after=fin2,
        out_specs=ANY,
    )(pos, kept_self, got_self, message, units[0, 0][1], fin0, fin1, back0, back1)
    return call(
        "place",
        place_kernel,
        [out_shape],
        [SMEM, ANY, VMEM, VMEM],
        [pltpu.SemaphoreType.DMA((8,))],
        out_specs=ANY,
        aliases={1: 0},
    )(pos, out, fin2, back2)


def solution(mesh):
    return jax.shard_map(
        shards,
        mesh=mesh,
        in_specs=(P(None, "rows", None, None, "freq"), P("rows", None)),
        out_specs=P(None, "rows", None, "freq", None),
        check_vma=False,
    )
```

```python
import jax
import jax.numpy as jnp
from jax import lax
from jax.experimental import pallas as pl
from jax.experimental.pallas import tpu as pltpu
from jax.sharding import PartitionSpec as P

TS = 512
HALF = 256
BAND = 4
CHUNKS = 2
CR = HALF // CHUNKS
TILES = 4
ROWS = 2 * BAND * 2 * CR
EPSILON = 1e-06
TINY = 1e-30
CODE = 2.0**7.5
VMEM = pl.BlockSpec(memory_space=pltpu.VMEM)
ANY = pl.BlockSpec(memory_space=pl.ANY)
SMEM = pl.BlockSpec(memory_space=pltpu.SMEM)
MIB = 1024 * 1024
PCOST = 0
TCOST = 2**32
FCOST = 2**35


def encode(x):
    u = x * CODE
    y = u * u
    y = y * y
    y = y * y
    y = y * y
    return jnp.where(u < 0, -y, y).astype(jnp.bfloat16)


def decode(y):
    y = y.astype(jnp.float32)
    r = lax.rsqrt(lax.rsqrt(lax.rsqrt(lax.rsqrt(jnp.abs(y))))) * (1.0 / CODE)
    return jnp.where(y < 0, -r, r)


def column(row):
    width = row.shape[1]
    return jnp.transpose(jnp.broadcast_to(row, (128, width)))


def tile_rows(part, tile):
    return pl.ds((part * 2 + tile) * CR, CR)


def put_energies(messages, given_ref):
    for i, message in enumerate(messages):
        rest = message
        for level in range(3):
            term = rest.astype(jnp.bfloat16)
            rest = rest - term.astype(jnp.float32)
            for h in range(2):
                row = TILES * CR + (i * 3 + level) * 2 + h
                given_ref[row : row + 1, :] = term[:, h * HALF : h * HALF + HALF]


def get_energy(got_ref, i):
    tail = got_ref[TILES * CR :, :].astype(jnp.float32)
    halves = []
    for h in range(2):
        rows = [tail[(i * 3 + level) * 2 + h :][:1] for level in range(3)]
        halves.append(rows[0] + (rows[1] + rows[2]))
    return jnp.concatenate(halves, axis=1)


def inverse(energy):
    return lax.rsqrt(jnp.maximum(energy, TINY))


def chunk_of_lanes(row, j):
    return jnp.concatenate(
        [row[:, h * HALF + j * CR : h * HALF + j * CR + CR] for h in range(2)], axis=1
    )


def complex_product(left, right_re, right_im):
    rows = left.shape[0] // 2
    real, imag = left[:rows], left[rows:]
    both = jnp.concatenate(
        [jnp.concatenate([real, imag], axis=1), jnp.concatenate([imag, -real], axis=1)], axis=0
    )
    right = jnp.concatenate([right_re, right_im], axis=1)
    product = lax.dot_general(
        both, right, (((1,), (1,)), ((), ())), preferred_element_type=jnp.float32
    )
    return product[:rows], product[rows:]


def live_before(band_ref, tile):
    return sum((band_ref[0, d] < tile).astype(jnp.int32) for d in range(BAND))


def run(copies):
    for copy in copies:
        copy.start()
    for copy in copies:
        copy.wait()


def pack_kernel(pos_ref, tiles_ref, own_ref, chunk0_ref, token_ref, shift_ref, band_ref, sem):
    bands = pltpu.make_async_copy(tiles_ref, band_ref, sem.at[17])
    bands.start()
    copies = [
        pltpu.make_async_copy(
            own_ref.at[part, d, pl.ds(half * HALF, CR), :],
            chunk0_ref.at[pl.ds(((part * BAND + d) * 2 + half) * CR, CR), :],
            sem.at[(part * BAND + d) * 2 + half],
        )
        for part in range(2)
        for d in range(BAND)
        for half in range(2)
    ]
    for copy in copies:
        copy.start()
    token_ref[...] = jnp.zeros_like(token_ref)
    shift_ref[...] = jnp.zeros_like(shift_ref)
    bands.wait()
    for offset in (1, 2):
        count = live_before(band_ref, pos_ref[2] + offset).astype(jnp.float32)
        shift_ref[offset : offset + 1, :] = jnp.full((1, HALF), count).astype(jnp.bfloat16)
    run([pltpu.make_async_copy(shift_ref, chunk0_ref.at[pl.ds(ROWS, 16), :], sem.at[16])])
    for copy in copies:
        copy.wait()


def order_kernel(*refs):
    token_ref = refs[-1]
    token_ref[...] = jnp.zeros_like(token_ref)


def second_kernel(own_ref, chunk1_ref):
    for part in range(2):
        for d in range(BAND):
            for half in range(2):
                row = ((part * BAND + d) * 2 + half) * CR
                start = half * HALF + CR
                chunk1_ref[row : row + CR, :] = own_ref[part, d, start : start + CR, :]


def self_kernel(
    pos_ref, own_ref, kept_ref, given_ref, msg_ref, again_ref, product_ref, col_ref, sem
):
    mine = pos_ref[1]
    again = pltpu.make_async_copy(own_ref, again_ref, sem)
    again.start()
    msg_ref[...] = jnp.zeros_like(msg_ref)
    right_re = jnp.concatenate([own_ref[0, d] for d in range(BAND)], axis=1)
    right_im = jnp.concatenate([own_ref[1, d] for d in range(BAND)], axis=1)
    diagonal = lax.broadcasted_iota(jnp.int32, (HALF, HALF), 0) == lax.broadcasted_iota(
        jnp.int32, (HALF, HALF), 1
    )
    for half in range(2):
        start = half * HALF
        left = jnp.concatenate(
            [
                jnp.concatenate(
                    [own_ref[part, d, start : start + HALF, :] for d in range(BAND)], axis=1
                )
                for part in range(2)
            ],
            axis=0,
        )
        real, imag = complex_product(left, right_re, right_im)
        product_ref[half, 0] = real
        product_ref[half, 1] = imag
        energies = jnp.where(diagonal, real[:, start : start + HALF], 0.0)
        msg_ref[0:1, start : start + HALF] = jnp.sum(energies, axis=0, keepdims=True)
        col_ref[start : start + HALF, :] = jnp.broadcast_to(
            jnp.sum(energies, axis=1, keepdims=True), (HALF, 128)
        )
    other = pl.multiple_of((1 - mine) * HALF, HALF)
    scale = lax.rsqrt(jnp.maximum(col_ref[pl.ds(other, HALF), 0:1], TINY)) * lax.rsqrt(
        jnp.maximum(msg_ref[0:1, :], TINY)
    )
    for part in range(2):
        given_ref[part] = encode(product_ref[1 - mine, part] * scale)
        kept_ref[part] = product_ref[mine, part]
    again.wait()


def row_energies(load, blocks):
    rows = []
    for block in range(blocks):
        total = jnp.zeros((CR, HALF), jnp.float32)
        for part in range(2):
            for d in range(BAND):
                wide = load(part, d, block).astype(jnp.float32)
                total += wide * wide
        folded = jnp.transpose(total[:, :128] + total[:, 128:])
        rows.append(jnp.sum(folded, axis=0, keepdims=True))
    return jnp.concatenate(rows, axis=1)


def pair_kernel(j, unit, pos_ref, band_ref, own_ref, far_ref, shift_ref, own_m, *rest):
    if (j, unit) == (0, 0):
        kept_ref, given_ref, pair_m, col_ref = rest
        pair_m[...] = jnp.zeros_like(pair_m)
    else:
        before_m, *rest = rest
        if unit == 1:
            near_ref, *rest = rest
        kept_ref, given_ref, pair_m, col_ref = rest
        pair_m[...] = before_m[...]
    core = pos_ref[0]
    mine = pos_ref[1]

    def far_block(part, k, half):
        start = pl.multiple_of(((part * BAND + k) * 2 + half) * CR, CR)
        return far_ref[pl.ds(start, CR), :]

    def far_chunk(part, k):
        start = pl.multiple_of((part * BAND + k) * 2 * CR, 2 * CR)
        return far_ref[pl.ds(start, 2 * CR), :]

    if unit == 0:
        pair_m[1:2, : 2 * CR] = row_energies(far_block, 2)
    elif j == 0:
        pair_m[0:1, :] = row_energies(
            lambda part, d, block: near_ref[part, d, block * CR : block * CR + CR, :], TS // CR
        )
    own_row = own_m[0:1, :]
    near_row = pair_m[0:1, :]
    far_row = pair_m[1:2, : 2 * CR]
    given_ref[TILES * CR :, :] = jnp.zeros((32, HALF), jnp.bfloat16)
    put_energies((own_row, near_row, pair_m[1:2, :]), given_ref)

    def aligned(load, part, s):
        blocks = []
        for d in range(BAND):
            block = load(part, jnp.maximum(d - s, 0))
            if d < 2:
                block = jnp.where(d >= s, block, jnp.zeros_like(block))
            blocks.append(block)
        return jnp.concatenate(blocks, axis=1)

    def chunk_of_rows(ref):
        def load(part, k):
            return jnp.concatenate(
                [ref[part, k, h * HALF + j * CR : h * HALF + j * CR + CR, :] for h in range(2)],
                axis=0,
            )
        return load

    def emit(keep, real, imag, start, rows, row, split):
        for part, value in enumerate((real, imag)):
            if not keep:
                value = encode(value * (col_ref[pl.ds(start, rows), 0:1] * row))
            for tile in range(2):
                if keep:
                    kept_ref[part, tile] = split(value, tile)
                else:
                    given_ref[tile_rows(part, tile), :] = split(value, tile)

    @pl.when(core == 0)
    def _():
        col_ref[...] = column(inverse(own_row))
        if unit == 0:
            load, energy = far_chunk, far_row
        else:
            load, energy = chunk_of_rows(near_ref), chunk_of_lanes(near_row, j)
        s = live_before(band_ref, pos_ref[2] + 2 - unit)
        right_re = aligned(load, 0, s)
        right_im = aligned(load, 1, s)
        row = inverse(energy)
        for keep in (False, True):
            start = pl.multiple_of((mine if keep else 1 - mine) * HALF, HALF)
            left = jnp.concatenate(
                [
                    jnp.concatenate(
                        [own_ref[part, d, pl.ds(start, HALF), :] for d in range(BAND)], axis=1
                    )
                    for part in range(2)
                ],
                axis=0,
            )
            real, imag = complex_product(left, right_re, right_im)
            emit(keep, real, imag, start, HALF, row, lambda v, t: v[t * CR : t * CR + CR])

    @pl.when(core == 1)
    def _():
        col_ref[: 2 * CR, :] = column(inverse(far_row))
        shifts = shift_ref[ROWS:, :].astype(jnp.float32)
        right_ref, energy = (own_ref, own_row) if unit == 0 else (near_ref, near_row)
        s = jnp.max(shifts[2 - unit : 3 - unit, :]).astype(jnp.int32)
        load = lambda part, k: right_ref[part, k]
        right_re = aligned(load, 0, s)
        right_im = aligned(load, 1, s)
        row = inverse(energy)
        for keep in (False, True):
            half = mine if keep else 1 - mine
            left = jnp.concatenate(
                [
                    jnp.concatenate([far_block(part, d, half) for d in range(BAND)], axis=1)
                    for part in range(2)
                ],
                axis=0,
            )
            real, imag = complex_product(left, right_re, right_im)
            start = pl.multiple_of(half * CR, CR)
            emit(keep, real, imag, start, CR, row, lambda v, t: v[:, t * HALF : t * HALF + HALF])


def decode_kernel(j, units, pos_ref, own_m, pair_m, *rest):
    kepts = rest[: len(units)]
    gots = rest[len(units) : 2 * len(units)]
    fin_ref, col_ref = rest[2 * len(units) :]
    core = pos_ref[0]
    mine = pos_ref[1]
    for n, (unit, kept_ref, got_ref) in enumerate(zip(units, kepts, gots)):
        other = [get_energy(got_ref, i) for i in range(3)]
        total = [m + o for m, o in zip((own_m[0:1, :], pair_m[0:1, :], pair_m[1:2, :]), other)]
        root = [jnp.sqrt(jnp.maximum(o, TINY)) for o in other]

        def emit(tile, start, root_row, total_row):
            back = col_ref[0, pl.ds(start, CR), 0:1] * root_row
            scale = lax.rsqrt(col_ref[1, pl.ds(start, CR), 0:1] * total_row + EPSILON)
            for part in range(2):
                value = kept_ref[part, tile] + decode(got_ref[tile_rows(part, tile), :]) * back
                fin_ref[n, part, tile] = (value * scale).astype(jnp.bfloat16)

        @pl.when(core == 0)
        def _():
            col_ref[0] = column(root[0])
            col_ref[1] = column(total[0])
            for tile in range(2):
                start = pl.multiple_of(mine * HALF + tile * CR, CR)
                if unit == 0:
                    emit(tile, start, root[2][:, : 2 * CR], total[2][:, : 2 * CR])
                else:
                    emit(tile, start, chunk_of_lanes(root[1], j), chunk_of_lanes(total[1], j))

        @pl.when(core == 1)
        def _():
            col_ref[0] = column(root[2])
            col_ref[1] = column(total[2])
            start = pl.multiple_of(mine * CR, CR)
            i = 0 if unit == 0 else 1
            for tile in range(2):
                lanes = slice(tile * HALF, tile * HALF + HALF)
                emit(tile, start, root[i][:, lanes], total[i][:, lanes])


def place_copies(core, j, unit, source_ref, out_ref, sem):
    copies = []
    for part in range(2):
        for tile in range(2):
            at = out_ref.at[part, 0, 2 - unit]
            piece = source_ref.at[part, tile]
            n = part * 2 + tile
            if core == 1:
                target = at.at[pl.ds(j * CR, CR), pl.ds(tile * HALF, HALF)]
                copies.append(pltpu.make_async_copy(piece, target, sem.at[n]))
            else:
                for h in range(2):
                    target = at.at[pl.ds(tile * CR, CR), pl.ds(h * HALF + j * CR, CR)]
                    source = piece.at[:, pl.ds(h * CR, CR)]
                    copies.append(pltpu.make_async_copy(source, target, sem.at[2 * n + h]))
    return copies


def finish_kernel(
    pos_ref, kept_ref, got_ref, mine_ref, first_ref, fin0, fin1, back0, back1,
    out_ref, fin_ref, col_ref, sem, place_sem,
):
    places = ((0, 0, 0, 0), (0, 1, 0, 1), (1, 0, 1, 0))
    for wait in (False, True):
        for core, sources in enumerate(((fin0, fin1), (back0, back1))):
            @pl.when(pos_ref[0] == core)
            def _():
                for n, (j, unit, source, slot) in enumerate(places):
                    for copy in place_copies(
                        core, j, unit, sources[source].at[slot], out_ref, place_sem.at[n]
                    ):
                        if wait:
                            copy.wait()
                        else:
                            copy.start()
        if wait:
            break
        start = pl.multiple_of(pos_ref[1] * HALF, HALF)
        energy = get_energy(first_ref, 0)
        other = jnp.sqrt(jnp.maximum(energy, TINY))
        total = mine_ref[0:1, :] + energy
        col_ref[0] = column(other)
        col_ref[1] = column(total)
        scale = lax.rsqrt(col_ref[1, pl.ds(start, HALF), 0:1] * total + EPSILON)
        back = col_ref[0, pl.ds(start, HALF), 0:1] * other
        for part in range(2):
            value = (kept_ref[part] + decode(got_ref[part]) * back) * scale
            fin_ref[part] = value.astype(jnp.bfloat16)
        run(
            [
                pltpu.make_async_copy(fin_ref.at[part], out_ref.at[part, 0, 0], sem.at[part])
                for part in range(2)
            ]
        )


def place_kernel(pos_ref, out_in_ref, fin_ref, back_ref, out_ref, sem):
    del out_in_ref
    for core, source in enumerate((fin_ref, back_ref)):
        @pl.when(pos_ref[0] == core)
        def _():
            run(place_copies(core, 1, 1, source.at[0], out_ref, sem))


def call(name, kernel, outs, specs, scratch=(), flops=0, after=None, out_specs=None, aliases=None, vmem=40):
    shapes = [jax.ShapeDtypeStruct(shape, dtype) for shape, dtype in outs]
    body = kernel if after is None else lambda _, *refs: kernel(*refs)
    run = pl.pallas_call(
        body,
        name=name,
        out_shape=shapes if len(shapes) > 1 else shapes[0],
        in_specs=specs if after is None else [ANY, *specs],
        out_specs=out_specs or ([VMEM] * len(shapes) if len(shapes) > 1 else VMEM),
        scratch_shapes=list(scratch),
        compiler_params=pltpu.CompilerParams(vmem_limit_bytes=vmem * MIB),
        input_output_aliases=aliases or {},
        cost_estimate=pl.CostEstimate(flops=flops, bytes_accessed=2**21, transcendentals=0),
    )
    return run if after is None else lambda *args: run(after, *args)


def shards(correlation, band_tiles):
    bf16, f32 = jnp.bfloat16, jnp.float32
    count = lax.axis_size("rows")
    core = lax.axis_index("rows") % 2
    mine = lax.axis_index("freq") % 2
    pos = jnp.stack([core, mine, lax.axis_index("rows")]).astype(jnp.int32)
    own = correlation.reshape(2, BAND, TS, HALF)
    swap = [(i, i ^ 1) for i in range(lax.axis_size("freq"))]
    pair = [(i, i ^ 1) for i in range(count)]
    far_route = [(i + 2, i) for i in range(0, count - 2, 2)] + [(i - 2, i) for i in range(3, count, 2)]
    back_route = [(i, i - 2) for i in range(3, count, 2)]

    half_shape = (2, HALF, TS)
    token = ((8, 128), f32)
    chunk0, after = call(
        "pack",
        pack_kernel,
        [((ROWS + 16, HALF), bf16), token],
        [SMEM, ANY, ANY],
        [pltpu.VMEM((16, HALF), bf16), pltpu.SMEM((1, BAND), jnp.int32), pltpu.SemaphoreType.DMA((18,))],
        vmem=52,
    )(pos, band_tiles, own)
    far0 = lax.ppermute(chunk0, "rows", far_route)
    kept_self, given_self, message, again = call(
        "self",
        self_kernel,
        [(half_shape, f32), (half_shape, bf16), ((8, TS), f32), (own.shape, bf16)],
        [SMEM, VMEM],
        [
            pltpu.VMEM((2, 2, HALF, TS), f32),
            pltpu.VMEM((TS, 128), f32),
            pltpu.SemaphoreType.DMA(()),
        ],
        after=after,
    )(pos, own)
    got_self = lax.ppermute(given_self, "freq", swap)
    chunk1 = call(
        "second",
        second_kernel,
        [((ROWS, HALF), bf16)],
        [VMEM],
        after=given_self,
    )(own)
    far1 = lax.ppermute(chunk1, "rows", far_route)
    near = lax.ppermute(again, "rows", pair)
    far = (far0, far1)

    unit_shape = (2, 2, CR, HALF)
    after = call("order", order_kernel, [token], [ANY], flops=TCOST)(far0)
    units = {}
    pair_m = None
    def finished(name, j, which, after):
        kepts = [units[j, unit][0] for unit in which]
        gots = [units[j, unit][1] for unit in which]
        fin = call(
            name,
            lambda *refs: decode_kernel(j, which, *refs),
            [((len(which), *unit_shape), bf16)],
            [SMEM] + [VMEM] * (2 + 2 * len(which)),
            [pltpu.VMEM((2, TS, 128), f32)],
            after=after,
        )(pos, message, units[j, which[-1]][2], *kepts, *gots)
        return fin, lax.ppermute(fin, "rows", back_route)

    for j in range(CHUNKS):
        for unit in range(2):
            if (j, unit) == (1, 1):
                fin0, back0 = finished("decode0", 0, (0, 1), after)
                after = fin0
            extra = [] if pair_m is None else [pair_m] + [near] * unit
            kept, given, pair_m = call(
                f"pair{j}{unit}",
                lambda *refs, j=j, unit=unit: pair_kernel(j, unit, *refs),
                [(unit_shape, f32), ((TILES * CR + 32, HALF), bf16), ((8, TS), f32)],
                [SMEM, SMEM] + [VMEM] * (4 + len(extra)),
                [pltpu.VMEM((TS, 128), f32)],
                flops=PCOST,
                after=after,
            )(pos, band_tiles, own, far[j], far0, message, *extra)
            units[j, unit] = kept, lax.ppermute(given, "freq", swap), pair_m
            after = kept
            if (j, unit) == (0, 0):
                after = call("order1", order_kernel, [token], [ANY], flops=FCOST, after=kept)(got_self)

    fin1, back1 = finished("decode1", 1, (0,), after)
    fin2, back2 = finished("decode2", 1, (1,), fin1)
    out_shape = ((2, 1, 3, HALF, TS), bf16)
    out = call(
        "finish",
        finish_kernel,
        [out_shape],
        [SMEM] + [VMEM] * 8,
        [
            pltpu.VMEM((2, HALF, TS), bf16),
            pltpu.VMEM((2, TS, 128), f32),
            pltpu.SemaphoreType.DMA((2,)),
            pltpu.SemaphoreType.DMA((3, 8)),
        ],
        after=fin2,
        out_specs=ANY,
    )(pos, kept_self, got_self, message, units[0, 0][1], fin0, fin1, back0, back1)
    return call(
        "place",
        place_kernel,
        [out_shape],
        [SMEM, ANY, VMEM, VMEM],
        [pltpu.SemaphoreType.DMA((8,))],
        out_specs=ANY,
        aliases={1: 0},
    )(pos, out, fin2, back2)


def solution(mesh):
    return jax.shard_map(
        shards,
        mesh=mesh,
        in_specs=(P(None, "rows", None, None, "freq"), P("rows", None)),
        out_specs=P(None, "rows", None, "freq", None),
        check_vma=False,
    )
```
